128 devices in a mesh: dp: 8 (over z, core), mp: 16 (over x, y).
Axes of the slice: x: 4, y: 4, z: 4, core: 2. Of those that a mesh axis runs over, the one named last changes fastest.
Arguments:
- gradient: bfloat16 [8, 8192, 8192], P('dp', 'mp'), may hold values from -6 to 6
- error: bfloat16 [8, 8192, 8192], P('dp', 'mp'), may hold values from -4 to 4
- query: bfloat16 [8192, 256], P('mp'), may hold values from -0.0625 to 0.0625
Outputs:
- factor: float32 [8192, 256], P('mp')
- new_error: bfloat16 [8, 8192, 8192], P('dp', 'mp')
The draws below stay inside these ranges and needn't reach their ends.
All inputs are finite; a program needn't handle non-finite values.
Results may differ from the reference program's by a relative error of at most 0.013.
Values may be sent and summed in bfloat16 or wider, within the bound.
No kernel may reach another device: no remote copies, remote signals or barrier semaphores. Data moves between devices by JAX's collectives and lax.ppermute only.
A program may use at most 128 MiB of HBM per device.

```python
import jax
import jax.numpy as jnp
from jax import lax

ROWS = 8192
COLS = 8192
RANK = 256
REPLICAS = 8
N_DP = 8


def levels(own_key, extent, shards, least, top_value):
    level, own = 1.0, jax.random.fold_in(own_key, 6)
    for position, blocks in shards:
        heights = jnp.exp(jax.random.uniform(jax.random.fold_in(own, position), (blocks,), jnp.float32, least / len(shards), top_value / len(shards)))
        level = level * jnp.repeat(heights, extent[position] // blocks).reshape([-1 if axis == position else 1 for axis in range(len(extent))])
    return level


def noise(key, shape, width, reach, cuts=(), held_as=jnp.bfloat16):
    factor_of = levels(key, shape, cuts, -0.22, 0.18) if cuts else 1.0
    result = jax.random.normal(key, shape, jnp.float32) * width * factor_of
    return jnp.minimum(jnp.maximum(result, -reach), reach).astype(held_as)


def setup_inputs(seed: int = 0) -> dict:
    seeds = jax.random.split(jax.random.key(seed), 4)
    return {
        "gradient": noise(seeds[0], (REPLICAS, ROWS, COLS), 1.0, 6.0, ((0, 8), (1, 16))),
        "error": noise(seeds[1], (REPLICAS, ROWS, COLS), 0.5, 4.0, ((0, 8), (1, 16))),
        "query": noise(seeds[2], (COLS, RANK), COLS ** -0.5, 0.0625, ((0, 16),)),
    }


def reference(gradient, error, query):
    adjusted = (gradient.astype(jnp.float32) + error.astype(jnp.float32)).astype(jnp.bfloat16)
    projections = lax.map(lambda block: jnp.dot(block.astype(jnp.float32), query.astype(jnp.float32), preferred_element_type=jnp.float32), adjusted)
    summed = jnp.sum(projections, axis=0)
    gram = jnp.dot(summed.T, summed, precision=lax.Precision.HIGHEST)
    lower = jnp.linalg.cholesky(gram)
    basis = lax.linalg.triangular_solve(lower, summed, left_side=False, lower=True, transpose_a=True).astype(jnp.bfloat16)
    terms = lax.map(lambda block: lax.dot_general(block.astype(jnp.float32), basis.astype(jnp.float32), (((0,), (0,)), ((), ())), preferred_element_type=jnp.float32), adjusted)
    factor = jnp.sum(terms, axis=0) / N_DP
    factor_half = factor.astype(jnp.bfloat16)
    approx = lax.dot_general(basis.astype(jnp.float32), factor_half.astype(jnp.float32), (((1,), (1,)), ((), ())), preferred_element_type=jnp.float32)
    new_error = (adjusted.astype(jnp.float32) - approx[None]).astype(jnp.bfloat16)
    return (factor, new_error)
```

```python
import jax
import jax.numpy as jnp
from jax import lax
from jax.experimental import pallas as pl
from jax.experimental.pallas import tpu as pltpu
from jax.sharding import Mesh, PartitionSpec as P

BF16 = jnp.bfloat16
F32 = jnp.float32
VMEM_LIMIT = 48 * 1024 * 1024
ROWS, COLS, RANK = 512, 8192, 256
NZ, NM = 4, 16
HALF = COLS // 2
BLK = COLS // NM
SUB = BLK // 2
TN_DOT = (((0,), (0,)), ((), ()))

SMEM = pl.BlockSpec(memory_space=pltpu.SMEM)


def params(**kw):
    return pltpu.CompilerParams(vmem_limit_bytes=VMEM_LIMIT, **kw)


def pick(c, first, second):
    return jnp.where(c == 0, first, second)


def adjust_kernel(c_ref, g_ref, e_ref, own_ref, other_ref):
    c = c_ref[0]
    a = (g_ref[...].astype(F32) + e_ref[...].astype(F32)).astype(BF16)
    shards = a.shape[1] // BLK
    for ref, flip in ((own_ref, 0), (other_ref, 1)):
        for s in range(shards):
            lo = a[:, s * BLK : s * BLK + SUB]
            hi = a[:, s * BLK + SUB : (s + 1) * BLK]
            ref[:, s * SUB : (s + 1) * SUB] = pick(c, (lo, hi)[flip], (hi, lo)[flip])


def adjust(c, gradient, error):
    steps = 8
    wide = pl.BlockSpec((ROWS, COLS // steps), lambda j: (0, j))
    half = pl.BlockSpec((ROWS, HALF // steps), lambda j: (0, j))
    out = jax.ShapeDtypeStruct((ROWS, HALF), BF16)
    return pl.pallas_call(
        adjust_kernel,
        grid=(steps,),
        in_specs=[SMEM, wide, wide],
        out_specs=[half, half],
        out_shape=[out, out],
        compiler_params=params(),
        cost_estimate=pl.CostEstimate(flops=ROWS * COLS, bytes_accessed=6 * ROWS * COLS, transcendentals=0),
    )(c, gradient, error)


def project_kernel(c_ref, a_ref, b_ref, q_ref, keep_ref, give_ref, acc):
    step = pl.program_id(0)

    @pl.when(step == 0)
    def _():
        acc[...] = jnp.zeros_like(acc)

    q = q_ref[...]
    acc[...] += jnp.dot(a_ref[...], q, preferred_element_type=F32)
    acc[...] += jnp.dot(b_ref[...], q, preferred_element_type=F32)

    @pl.when(step == pl.num_programs(0) - 1)
    def _():
        c = c_ref[0]
        h = ROWS // 2
        keep_ref[...] = acc[pl.ds(c * h, h), :]
        give_ref[...] = acc[pl.ds((1 - c) * h, h), :]


def project(c, own, recv, query):
    steps = 4
    a = pl.BlockSpec((ROWS, HALF // steps), lambda j: (0, j))
    q = pl.BlockSpec((HALF // steps, RANK), lambda j: (j, 0))
    o = pl.BlockSpec((ROWS // 2, RANK), lambda j: (0, 0))
    out = jax.ShapeDtypeStruct((ROWS // 2, RANK), F32)
    return pl.pallas_call(
        project_kernel,
        grid=(steps,),
        in_specs=[SMEM, a, a, q],
        out_specs=[o, o],
        out_shape=[out, out],
        scratch_shapes=[pltpu.VMEM((ROWS, RANK), F32)],
        compiler_params=params(),
        cost_estimate=pl.CostEstimate(flops=4 * ROWS * HALF * RANK, bytes_accessed=4 * ROWS * HALF + 2 * HALF * RANK, transcendentals=0),
    )(c, own, recv, query)


def term_kernel(c_ref, s_ref, a_ref, b_ref, t_ref, g_ref):
    s = s_ref[...]
    t = lax.dot_general(s, a_ref[...], TN_DOT, preferred_element_type=F32)
    t += lax.dot_general(s, b_ref[...], TN_DOT, preferred_element_type=F32)
    t_ref[0] = t.astype(BF16).reshape(NM, RANK // NM, HALF // NZ)

    @pl.when(pl.program_id(0) == 0)
    def _():
        g = lax.dot_general(s, s, TN_DOT, preferred_element_type=F32)
        h = RANK // 2
        g_ref[...] = pick(c_ref[0], g[:h], g[h:])


def term(c, summed, own, recv):
    a = pl.BlockSpec((ROWS, HALF // NZ), lambda j: (0, j))
    return pl.pallas_call(
        term_kernel,
        grid=(NZ,),
        in_specs=[SMEM, pl.BlockSpec((ROWS, RANK), lambda j: (0, 0)), a, a],
        out_specs=[
            pl.BlockSpec((1, NM, RANK // NM, HALF // NZ), lambda j: (j, 0, 0, 0)),
            pl.BlockSpec((RANK // 2, RANK), lambda j: (0, 0)),
        ],
        out_shape=[
            jax.ShapeDtypeStruct((NZ, NM, RANK // NM, HALF // NZ), BF16),
            jax.ShapeDtypeStruct((RANK // 2, RANK), F32),
        ],
        compiler_params=params(),
        cost_estimate=pl.CostEstimate(flops=4 * ROWS * HALF * RANK, bytes_accessed=4 * ROWS * HALF + 2 * HALF * RANK, transcendentals=0),
    )(c, summed, own, recv)


def total_kernel(x_ref, o_ref):
    n = x_ref.shape[0]
    total = jnp.sum(x_ref[...].astype(F32), axis=0).astype(BF16)
    o_ref[...] = jnp.broadcast_to(total[None], (n,) + total.shape)


def total(pieces):
    return pl.pallas_call(
        total_kernel,
        in_specs=[pl.BlockSpec(memory_space=pltpu.VMEM)],
        out_specs=pl.BlockSpec(memory_space=pltpu.VMEM),
        out_shape=jax.ShapeDtypeStruct(pieces.shape, BF16),
        compiler_params=params(),
        cost_estimate=pl.CostEstimate(flops=pieces.size, bytes_accessed=4 * pieces.size, transcendentals=0),
    )(pieces)


def finish_kernel(c_ref, m_ref, w_ref, inv_ref, own_ref, other_ref, t_ref, u_ref, err_ref, f_ref):
    c, m = c_ref[0], m_ref[0]
    w = w_ref[...]
    t = t_ref[0].reshape(RANK, HALF // NZ)
    u = u_ref[0].reshape(RANK, HALF // NZ)
    mine = own_ref[...].astype(F32) - jnp.dot(w, t, preferred_element_type=F32)
    theirs = other_ref[...].astype(F32) - jnp.dot(w, u, preferred_element_type=F32)
    mine, theirs = mine.astype(BF16), theirs.astype(BF16)
    shards = HALF // NZ // SUB
    for s in range(shards):
        x = mine[:, s * SUB : (s + 1) * SUB]
        y = theirs[:, s * SUB : (s + 1) * SUB]
        err_ref[:, s * BLK : s * BLK + SUB] = pick(c, x, y)
        err_ref[:, s * BLK + SUB : (s + 1) * BLK] = pick(c, y, x)

        @pl.when(pl.program_id(0) * shards + s == m)
        def _():
            cut = slice(s * SUB, (s + 1) * SUB)
            tm = pick(c, t[:, cut], u[:, cut]), pick(c, u[:, cut], t[:, cut])
            for k in range(2):
                f = jnp.dot(inv_ref[...], tm[k].astype(F32), precision=lax.Precision.HIGHEST, preferred_element_type=F32)
                f_ref[k * SUB : (k + 1) * SUB, :] = f.T * 0.125


def finish(c, m, w, inv, own, other, t, u):
    a = pl.BlockSpec((ROWS, HALF // NZ), lambda j: (0, j))
    tt = pl.BlockSpec((1, NM, RANK // NM, HALF // NZ), lambda j: (j, 0, 0, 0))
    return pl.pallas_call(
        finish_kernel,
        grid=(NZ,),
        in_specs=[
            SMEM,
            SMEM,
            pl.BlockSpec((ROWS, RANK), lambda j: (0, 0)),
            pl.BlockSpec((RANK, RANK), lambda j: (0, 0)),
            a,
            a,
            tt,
            tt,
        ],
        out_specs=[
            pl.BlockSpec((ROWS, COLS // NZ), lambda j: (0, j)),
            pl.BlockSpec((BLK, RANK), lambda j: (0, 0)),
        ],
        out_shape=[
            jax.ShapeDtypeStruct((ROWS, COLS), BF16),
            jax.ShapeDtypeStruct((BLK, RANK), F32),
        ],
        compiler_params=params(),
        cost_estimate=pl.CostEstimate(flops=2 * ROWS * COLS * RANK, bytes_accessed=4 * ROWS * COLS + 2 * COLS * RANK, transcendentals=0),
    )(c, m, w, inv, own, other, t, u)


def swap(x):
    return lax.ppermute(x, "c", [(0, 1), (1, 0)])


def ring_sum(x, axis):
    x1, x2, x3 = (lax.ppermute(x, axis, [(i, (i + k) % 4) for i in range(4)]) for k in (1, 2, 3))
    return (x.astype(F32) + x2.astype(F32)) + (x1.astype(F32) + x3.astype(F32))


def join(c, mine, theirs):
    return jnp.concatenate([pick(c, mine, theirs), pick(c, theirs, mine)], axis=0)


def shards(gradient, error, query):
    gradient, error = gradient[0], error[0]
    c = lax.axis_index("c")
    m = lax.axis_index("x") * 4 + lax.axis_index("y")
    cv, mv = c.reshape(1).astype(jnp.int32), m.reshape(1).astype(jnp.int32)

    with jax.named_scope("query_gather"):
        part = lax.dynamic_slice_in_dim(query, c * SUB, SUB, 0)
        copies = jnp.broadcast_to(part[None], (NM, SUB, RANK))
        half_query = lax.all_to_all(copies, ("x", "y"), 0, 0, tiled=True).reshape(HALF, RANK)

    with jax.named_scope("adjust"):
        own, other = adjust(cv, gradient, error)
        recv = swap(other)

    with jax.named_scope("project"):
        keep, give = project(cv, own, recv, half_query)
        chip = (keep + swap(give)).astype(BF16)
        rows = ring_sum(chip, "z").astype(BF16)
        summed = join(c, rows, swap(rows))

    with jax.named_scope("term"):
        pieces, gram_half = term(cv, summed, own, recv)
        pieces = pieces.reshape(NZ * NM, RANK // NM, HALF // NZ)
        pieces = lax.all_to_all(pieces, ("z", "x", "y"), 0, 0, tiled=True)

    with jax.named_scope("gram"):
        gram_half = ring_sum(ring_sum(gram_half, "x"), "y")
        gram = join(c, gram_half, swap(gram_half))
        lower = lax.linalg.cholesky(gram, symmetrize_input=False)
        inv = lax.linalg.triangular_solve(lower, jnp.eye(RANK, dtype=F32), left_side=True, lower=True)
        basis = lax.dot_general(summed.astype(F32), inv, (((1,), (1,)), ((), ())), precision=lax.Precision.HIGHEST)
        w = (jnp.dot(basis, inv, precision=lax.Precision.HIGHEST) * 0.125).astype(BF16)

    with jax.named_scope("gather"):
        mine = lax.all_to_all(total(pieces), ("z", "x", "y"), 0, 0, tiled=True)
        mine = mine.reshape(NZ, NM, RANK // NM, HALF // NZ)
        theirs = swap(mine)

    with jax.named_scope("finish"):
        new_error, factor = finish(cv, mv, w, inv, own, other, mine, theirs)
    return factor, new_error[None]


def solution(mesh):
    grid = Mesh(mesh.devices.reshape(4, 2, 4, 4), ("z", "c", "x", "y"))
    in_specs = (P(("z", "c"), ("x", "y"), None), P(("z", "c"), ("x", "y"), None), P(("x", "y"), None))
    out_specs = (P(("x", "y"), None), P(("z", "c"), ("x", "y"), None))
    return jax.shard_map(shards, mesh=grid, in_specs=in_specs, out_specs=out_specs, check_vma=False)
```

```python
import jax
import jax.numpy as jnp
from jax import lax
from jax.experimental import pallas as pl
from jax.experimental.pallas import tpu as pltpu
from jax.sharding import Mesh, PartitionSpec as P

BF16 = jnp.bfloat16
F32 = jnp.float32
VMEM_LIMIT = 40 * 1024 * 1024
ROWS, COLS, RANK = 512, 8192, 256
NZ, NM = 4, 16
HALF = COLS // 2
BLK = COLS // NM
SUB = BLK // 2
TN_DOT = (((0,), (0,)), ((), ()))

SMEM = pl.BlockSpec(memory_space=pltpu.SMEM)
VMEM = pl.BlockSpec(memory_space=pltpu.VMEM)
CHUNKS = 4
CHUNK = HALF // CHUNKS
STEP = 512
PER = CHUNK // STEP


def params(limit=VMEM_LIMIT):
    return pltpu.CompilerParams(vmem_limit_bytes=limit)


HBM = pl.BlockSpec(memory_space=pltpu.HBM)


def in_hbm(*arrays):
    return [pltpu.with_memory_space_constraint(x, pltpu.HBM) for x in arrays]


def load(pairs, sem, first=0):
    copies = [pltpu.make_async_copy(src, dst, sem.at[first + i]) for i, (src, dst) in enumerate(pairs)]
    for copy in copies:
        copy.start()
    return copies


class Stream:
    DEPTH = 3

    def __init__(self, groups, sem):
        self.groups, self.sem, self.started = groups, sem, []
        for _ in range(self.DEPTH):
            self.more()

    def more(self):
        k = len(self.started)
        if k < len(self.groups):
            self.started.append(load(self.groups[k], self.sem, sum(len(g) for g in self.groups[:k])))

    def get(self, k):
        for copy in self.started[k]:
            copy.wait()
        self.more()


def strip(width):
    return pl.BlockSpec((ROWS, width), lambda j: (0, j))


def chunk_strips():
    return [pl.BlockSpec((ROWS, STEP), lambda j, k=k: (0, jnp.clip(j - k * PER, 0, PER - 1))) for k in range(CHUNKS)]


def pick(c, first, second):
    return jnp.where(c == 0, first, second)


def adjust_kernel(c_ref, g_ref, e_ref, own_ref, *other_refs):
    c, step = c_ref[0], pl.program_id(0)
    a = (g_ref[...].astype(F32) + e_ref[...].astype(F32)).astype(BF16)
    for s in range(STEP // SUB):
        lo = a[:, s * BLK : s * BLK + SUB]
        hi = a[:, s * BLK + SUB : (s + 1) * BLK]
        own_ref[:, s * SUB : (s + 1) * SUB] = pick(c, lo, hi)
        other = pick(c, hi, lo)
        for k, ref in enumerate(other_refs):

            @pl.when(step // PER == k)
            def _():
                ref[:, s * SUB : (s + 1) * SUB] = other


def adjust(c, gradient, error):
    return pl.pallas_call(
        adjust_kernel,
        grid=(HALF // STEP,),
        in_specs=[SMEM, strip(2 * STEP), strip(2 * STEP)],
        out_specs=[strip(STEP)] + chunk_strips(),
        out_shape=[pltpu.HBM((ROWS, HALF), BF16)] + [pltpu.HBM((ROWS, CHUNK), BF16)] * CHUNKS,
        compiler_params=params(60 * 1024 * 1024),
        cost_estimate=pl.CostEstimate(flops=ROWS * COLS, bytes_accessed=6 * ROWS * COLS, transcendentals=0),
    )(c, gradient, error)


def pair_kernel(own_ref, *refs):
    chunks, o_ref = refs[:CHUNKS], refs[CHUNKS]
    for k, ref in enumerate(chunks):

        @pl.when(pl.program_id(0) // PER == k)
        def _():
            o_ref[...] = (own_ref[...].astype(F32) + ref[...].astype(F32)).astype(BF16)


def pair(own, chunks):
    return pl.pallas_call(
        pair_kernel,
        grid=(HALF // STEP,),
        in_specs=[strip(STEP)] + chunk_strips(),
        out_specs=strip(STEP),
        out_shape=pltpu.HBM((ROWS, HALF), BF16),
        compiler_params=params(60 * 1024 * 1024),
        cost_estimate=pl.CostEstimate(flops=ROWS * HALF, bytes_accessed=6 * ROWS * HALF, transcendentals=0),
    )(*in_hbm(own, *chunks))


def project_kernel(c_ref, q_ref, a_ref, keep_ref, give_ref, acc, a, sem):
    cuts = [slice(k * STEP, (k + 1) * STEP) for k in range(HALF // STEP)]
    stream = Stream([[(a_ref.at[:, cut], a.at[:, cut])] for cut in cuts], sem)
    for k, cut in enumerate(cuts):
        stream.get(k)
        x = jnp.dot(a[:, cut], q_ref[cut, :], preferred_element_type=F32)
        acc[...] = x if k == 0 else acc[...] + x
    c, h = c_ref[0], ROWS // 2
    keep_ref[...] = acc[pl.ds(pl.multiple_of(c * h, h), h), :]
    give_ref[...] = acc[pl.ds(pl.multiple_of((1 - c) * h, h), h), :]


def project(c, query, a):
    out = jax.ShapeDtypeStruct((ROWS // 2, RANK), F32)
    return pl.pallas_call(
        project_kernel,
        in_specs=[SMEM, VMEM, HBM],
        out_specs=[VMEM, VMEM],
        out_shape=[out, out],
        scratch_shapes=[
            pltpu.VMEM((ROWS, RANK), F32),
            pltpu.VMEM((ROWS, HALF), BF16),
            pltpu.SemaphoreType.DMA((HALF // STEP,)),
        ],
        compiler_params=params(),
        cost_estimate=pl.CostEstimate(flops=2 * ROWS * HALF * RANK, bytes_accessed=2 * ROWS * HALF + 2 * HALF * RANK, transcendentals=0),
    )(c, query, *in_hbm(a))


def gram_kernel(c_ref, mine_ref, theirs_ref, s_ref, st_ref, g_ref):
    c = c_ref[0]
    h = ROWS // 2
    x, y = mine_ref[...], theirs_ref[...]
    s_ref[:h, :] = pick(c, x, y)
    s_ref[h:, :] = pick(c, y, x)
    s = s_ref[...]
    st = s.T
    st_ref[...] = st
    r = RANK // 2
    g_ref[...] = jnp.dot(pick(c, st[:r], st[r:]), s, preferred_element_type=F32)


def gram_rows(c, mine, theirs):
    return pl.pallas_call(
        gram_kernel,
        grid=(1,),
        in_specs=[SMEM, VMEM, VMEM],
        out_specs=[pl.BlockSpec((ROWS, RANK), lambda j: (0, 0)), VMEM, VMEM],
        out_shape=[
            pltpu.HBM((ROWS, RANK), BF16),
            jax.ShapeDtypeStruct((RANK, ROWS), BF16),
            jax.ShapeDtypeStruct((RANK // 2, RANK), F32),
        ],
        compiler_params=params(),
        cost_estimate=pl.CostEstimate(flops=2 * ROWS * RANK * RANK, bytes_accessed=4 * ROWS * RANK, transcendentals=0),
    )(c, mine, theirs)


def term_kernel(st_ref, a_ref, t_ref, a, t, sem):
    cuts = [slice(k * STEP, (k + 1) * STEP) for k in range(HALF // STEP)]
    stream = Stream([[(a_ref.at[:, cut], a.at[:, cut])] for cut in cuts], sem)
    st = st_ref[...]
    wide = HALF // NZ
    per = wide // STEP
    sends = []
    for k, cut in enumerate(cuts):
        stream.get(k)
        x = jnp.dot(st, a[:, cut], preferred_element_type=F32)
        part = slice(k % per * STEP, (k % per + 1) * STEP)
        t[k // per, :, :, part] = x.astype(BF16).reshape(NM, RANK // NM, STEP)
        if k % per == per - 1:
            sends += load([(t.at[k // per], t_ref.at[k // per])], sem, len(cuts) + k // per)
    for send in sends:
        send.wait()


def term(st, a):
    return pl.pallas_call(
        term_kernel,
        in_specs=[VMEM, HBM],
        out_specs=HBM,
        out_shape=pltpu.HBM((NZ, NM, RANK // NM, HALF // NZ), BF16),
        scratch_shapes=[
            pltpu.VMEM((ROWS, HALF), BF16),
            pltpu.VMEM((NZ, NM, RANK // NM, HALF // NZ), BF16),
            pltpu.SemaphoreType.DMA((HALF // STEP + NZ,)),
        ],
        compiler_params=params(),
        cost_estimate=pl.CostEstimate(flops=2 * ROWS * HALF * RANK, bytes_accessed=2 * ROWS * HALF + 2 * HALF * RANK, transcendentals=0),
    )(st, *in_hbm(a))


def total_kernel(x_ref, o_ref, copy, sem):
    n, k = x_ref.shape[0], copy.shape[0]
    total = jnp.sum(x_ref[...].astype(F32), axis=0).astype(BF16)
    copy[...] = jnp.broadcast_to(total[None], copy.shape)
    for send in load([(copy, o_ref.at[pl.ds(i, k)]) for i in range(0, n, k)], sem):
        send.wait()


def total(pieces):
    k = 16
    return pl.pallas_call(
        total_kernel,
        in_specs=[VMEM],
        out_specs=HBM,
        out_shape=pltpu.HBM(pieces.shape, BF16),
        scratch_shapes=[
            pltpu.VMEM((k,) + pieces.shape[1:], BF16),
            pltpu.SemaphoreType.DMA((pieces.shape[0] // k,)),
        ],
        compiler_params=params(),
        cost_estimate=pl.CostEstimate(flops=pieces.size, bytes_accessed=4 * pieces.size, transcendentals=0),
    )(pieces)


def dot_hi(a, b, dims=(((1,), (0,)), ((), ()))):
    return lax.dot_general(a, b, dims, precision=lax.Precision.HIGHEST, preferred_element_type=F32)


NT_DOT = (((1,), (1,)), ((), ()))
BASE = 64


def inverse_factor(a):
    n = a.shape[0]
    if n > BASE:
        h = n // 2
        i11 = inverse_factor(a[:h, :h])
        l21 = dot_hi(a[h:, :h], i11, NT_DOT)
        i22 = inverse_factor(a[h:, h:] - dot_hi(l21, l21, NT_DOT))
        i21 = -dot_hi(i22, dot_hi(l21, i11))
        return jnp.concatenate(
            [jnp.concatenate([i11, jnp.zeros((h, h), F32)], axis=1), jnp.concatenate([i21, i22], axis=1)], axis=0
        )
    row = lax.broadcasted_iota(jnp.int32, (n, 2 * n), 0)
    lane = lax.broadcasted_iota(jnp.int32, (n, 2 * n), 1)
    x = jnp.concatenate([a, jnp.where(row == lane, 1.0, 0.0)[:, :n].astype(F32)], axis=1)
    for j in range(n - 1):
        column = jnp.broadcast_to(x[:, j : j + 1], x.shape)
        pivot = column[j : j + 1, :]
        ratio = jnp.where(row > j, column, 0.0) * (1.0 / pivot)
        x = x - ratio * x[j : j + 1, :]
    d = jnp.sum(jnp.where(row == lane, x, 0.0), axis=1, keepdims=True)
    return x[:, n:] * (1.0 / jnp.sqrt(d))


def solve_kernel(g_ref, s_ref, inv_ref, w_ref):
    inv = inverse_factor(g_ref[...])
    inv_ref[...] = inv
    basis = dot_hi(s_ref[...].astype(F32), inv, NT_DOT)
    w_ref[...] = (dot_hi(basis, inv) * 0.125).astype(BF16)


def solve(gram, summed):
    square = pl.BlockSpec((RANK, RANK), lambda j: (0, 0))
    tall = pl.BlockSpec((ROWS, RANK), lambda j: (0, 0))
    return pl.pallas_call(
        solve_kernel,
        grid=(1,),
        in_specs=[VMEM, tall],
        out_specs=[square, tall],
        out_shape=[pltpu.HBM((RANK, RANK), F32), pltpu.HBM((ROWS, RANK), BF16)],
        compiler_params=params(),
        cost_estimate=pl.CostEstimate(flops=2 * 10**10, bytes_accessed=10**6, transcendentals=0),
    )(gram, *in_hbm(summed))


def finish_kernel(c_ref, m_ref, w_ref, inv_ref, t_ref, u_ref, own_ref, *refs):
    chunks, (err_ref, f_ref, u, a, b, out, w_in, inv_in, sem) = refs[:CHUNKS], refs[CHUNKS:]
    c, m = c_ref[0], m_ref[0]
    wide = HALF // NZ
    n = HALF // STEP
    w_load, inv_load = load([(w_ref, w_in), (inv_ref, inv_in)], sem, 4 * n)
    groups = []
    for k in range(n):
        at, cut = k * STEP // wide, slice(k * STEP % wide, k * STEP % wide + STEP)
        half, part = slice(k * STEP, (k + 1) * STEP), slice(k % PER * STEP, (k % PER + 1) * STEP)
        groups.append(
            [
                (u_ref.at[at, :, :, cut], u.at[at, :, :, cut]),
                (own_ref.at[:, half], a.at[:, half]),
                (chunks[k // PER].at[:, part], b.at[:, half]),
            ]
        )
    stream = Stream(groups, sem)
    w_load.wait()
    inv_load.wait()
    w = w_in[...]
    sends = []
    for k in range(n):
        stream.get(k)
        at, cut = k * STEP // wide, slice(k * STEP % wide, k * STEP % wide + STEP)
        half = slice(k * STEP, (k + 1) * STEP)
        x = jnp.dot(w, t_ref[at, :, :, cut].reshape(RANK, STEP), preferred_element_type=F32)
        y = jnp.dot(w, u[at, :, :, cut].reshape(RANK, STEP), preferred_element_type=F32)
        x = (a[:, half].astype(F32) - x).astype(BF16)
        y = (b[:, half].astype(F32) - y).astype(BF16)
        base = 2 * k * STEP
        for s in range(STEP // SUB):
            part = slice(s * SUB, (s + 1) * SUB)
            out[:, base + s * BLK : base + s * BLK + SUB] = pick(c, x[:, part], y[:, part])
            out[:, base + s * BLK + SUB : base + (s + 1) * BLK] = pick(c, y[:, part], x[:, part])
        whole = slice(base, base + 2 * STEP)
        sends += load([(out.at[:, whole], err_ref.at[:, whole])], sem, 3 * n + k)
    per = wide // SUB
    cut = pl.ds(pl.multiple_of(m % per * SUB, SUB), SUB)
    x = t_ref[m // per, :, :, cut].reshape(RANK, SUB)
    y = u[m // per, :, :, cut].reshape(RANK, SUB)
    for k, part in enumerate((pick(c, x, y), pick(c, y, x))):
        f_ref[k * SUB : (k + 1) * SUB, :] = dot_hi(inv_in[...], part.astype(F32)).T * 0.125
    for send in sends:
        send.wait()


def finish(c, m, w, inv, own, others, t, u):
    return pl.pallas_call(
        finish_kernel,
        in_specs=[SMEM, SMEM, HBM, HBM, VMEM, HBM, HBM] + [HBM] * CHUNKS,
        out_specs=[HBM, VMEM],
        out_shape=[pltpu.HBM((ROWS, COLS), BF16), jax.ShapeDtypeStruct((BLK, RANK), F32)],
        scratch_shapes=[
            pltpu.VMEM((NZ, NM, RANK // NM, HALF // NZ), BF16),
            pltpu.VMEM((ROWS, HALF), BF16),
            pltpu.VMEM((ROWS, HALF), BF16),
            pltpu.VMEM((ROWS, COLS), BF16),
            pltpu.VMEM((ROWS, RANK), BF16),
            pltpu.VMEM((RANK, RANK), F32),
            pltpu.SemaphoreType.DMA((4 * HALF // STEP + 2,)),
        ],
        compiler_params=params(),
        cost_estimate=pl.CostEstimate(flops=2 * ROWS * COLS * RANK, bytes_accessed=4 * ROWS * COLS + 2 * COLS * RANK, transcendentals=0),
    )(c, m, *in_hbm(w, inv), t, *in_hbm(u, own, *others))


def swap(x):
    return lax.ppermute(x, "c", [(0, 1), (1, 0)])


def ring_sum(x, axis):
    x1, x2, x3 = (lax.ppermute(x, axis, [(i, (i + k) % 4) for i in range(4)]) for k in (1, 2, 3))
    return (x.astype(F32) + x2.astype(F32)) + (x1.astype(F32) + x3.astype(F32))


def join(c, mine, theirs):
    return jnp.concatenate([pick(c, mine, theirs), pick(c, theirs, mine)], axis=0)


def shards(gradient, error, query):
    gradient, error = gradient[0], error[0]
    c = lax.axis_index("c").astype(jnp.int32)
    m = (lax.axis_index("x") * 4 + lax.axis_index("y")).astype(jnp.int32)
    cv, mv = c.reshape(1), m.reshape(1)

    with jax.named_scope("query_gather"):
        part = lax.dynamic_slice_in_dim(query, c * SUB, SUB, 0)
        copies = jnp.broadcast_to(part[None], (NM, SUB, RANK))
        half_query = lax.all_to_all(copies, ("x", "y"), 0, 0, tiled=True).reshape(HALF, RANK)

    with jax.named_scope("adjust"):
        own, *others = adjust(cv, gradient, error)
        both = pair(own, [swap(other) for other in others])

    with jax.named_scope("project"):
        keep, give = project(cv, half_query, both)
        chip = (keep + swap(give)).astype(BF16)
        rows = ring_sum(chip, "z").astype(BF16)

    with jax.named_scope("gram"):
        summed, summed_t, gram_x = gram_rows(cv, rows, swap(rows))
        gram_x = ring_sum(gram_x, "x")

    with jax.named_scope("term"):
        pieces = term(summed_t, both).reshape(NZ * NM, RANK // NM, HALF // NZ)
        pieces, gram_x = lax.optimization_barrier((pieces, gram_x))
        pieces = lax.all_to_all(pieces, ("z", "x", "y"), 0, 0, tiled=True)

    with jax.named_scope("gather"):
        gram_y = ring_sum(gram_x, "y")
        pieces, gram_y = lax.optimization_barrier((pieces, gram_y))
        mine = lax.all_to_all(total(pieces), ("z", "x", "y"), 0, 0, tiled=True)

    with jax.named_scope("solve"):
        inv, w = solve(join(c, gram_y, swap(gram_y)), summed)
        mine, inv, w = lax.optimization_barrier((mine, inv, w))

    with jax.named_scope("finish"):
        mine = mine.reshape(NZ, NM, RANK // NM, HALF // NZ)
        new_error, factor = finish(cv, mv, w, inv, own, others, mine, swap(mine))
    return factor, new_error[None]


def solution(mesh):
    grid = Mesh(mesh.devices.reshape(4, 2, 4, 4), ("z", "c", "x", "y"))
    in_specs = (P(("z", "c"), ("x", "y"), None), P(("z", "c"), ("x", "y"), None), P(("x", "y"), None))
    out_specs = (P(("x", "y"), None), P(("z", "c"), ("x", "y"), None))
    return jax.shard_map(shards, mesh=grid, in_specs=in_specs, out_specs=out_specs, check_vma=False)
```

```python
import functools

import jax
import jax.numpy as jnp
from jax import lax
from jax.experimental import pallas as pl
from jax.experimental.pallas import tpu as pltpu
from jax.sharding import Mesh, PartitionSpec as P

BF16 = jnp.bfloat16
F32 = jnp.float32
VMEM_LIMIT = 40 * 1024 * 1024
ROWS, COLS, RANK = 512, 8192, 256
NZ, NM = 4, 16
HALF = COLS // 2
BLK = COLS // NM
SUB = BLK // 2
TN_DOT = (((0,), (0,)), ((), ()))

SMEM = pl.BlockSpec(memory_space=pltpu.SMEM)
VMEM = pl.BlockSpec(memory_space=pltpu.VMEM)
HBM = pl.BlockSpec(memory_space=pltpu.HBM)
CHUNKS = 4
CHUNK = HALF // CHUNKS
STEP = CHUNK // 2
STEPS = HALF // STEP
GROUP = RANK // NM


def params(limit=VMEM_LIMIT):
    return pltpu.CompilerParams(vmem_limit_bytes=limit)


def in_hbm(*arrays):
    return [pltpu.with_memory_space_constraint(x, pltpu.HBM) for x in arrays]


def load(pairs, sem, first=0):
    copies = [pltpu.make_async_copy(src, dst, sem.at[first + i]) for i, (src, dst) in enumerate(pairs)]
    for copy in copies:
        copy.start()
    return copies


class Stream:
    DEPTH = 4

    def __init__(self, groups, sem):
        self.groups, self.sem, self.started = groups, sem, []
        for _ in range(self.DEPTH):
            self.more()

    def more(self):
        k = len(self.started)
        if k < len(self.groups):
            self.started.append(load(self.groups[k], self.sem, sum(len(g) for g in self.groups[:k])))

    def get(self, k):
        for copy in self.started[k]:
            copy.wait()
        self.more()


def pick(c, first, second):
    return jnp.where(c == 0, first, second)


def adjust_kernel(c_ref, g_ref, d_ref, own_ref, *refs):
    chunks, (g, d, own, other, sem) = refs[:CHUNKS], refs[CHUNKS:]
    wide = [slice(2 * k * STEP, 2 * (k + 1) * STEP) for k in range(STEPS)]
    stream = Stream([[(g_ref.at[:, cut], g.at[k]), (d_ref.at[:, cut], d.at[k])] for k, cut in enumerate(wide)], sem)
    c = c_ref[0]
    sends = []
    for k in range(STEPS):
        stream.get(k)
        for s in range(STEP // SUB):
            part = slice(s * SUB, (s + 1) * SUB)
            for out, core in ((own, c), (other, 1 - c)):
                cut = pl.ds(pl.multiple_of(s * BLK + core * SUB, SUB), SUB)
                out[k, :, part] = (g[k, :, cut].astype(F32) + d[k, :, cut].astype(F32)).astype(BF16)
        cut = slice(k * STEP, (k + 1) * STEP)
        part = slice(k % 2 * STEP, (k % 2 + 1) * STEP)
        pairs = [(own.at[k], own_ref.at[:, cut]), (other.at[k], chunks[k // 2].at[:, part])]
        sends += load(pairs, sem, 2 * STEPS + 2 * k)
    for send in sends:
        send.wait()


def adjust(c, gradient, error):
    return pl.pallas_call(
        adjust_kernel,
        in_specs=[SMEM, HBM, HBM],
        out_specs=[HBM] * (1 + CHUNKS),
        out_shape=[pltpu.HBM((ROWS, HALF), BF16)] + [pltpu.HBM((ROWS, CHUNK), BF16)] * CHUNKS,
        scratch_shapes=[pltpu.VMEM((STEPS, ROWS, 2 * STEP), BF16)] * 2
        + [pltpu.VMEM((STEPS, ROWS, STEP), BF16)] * 2
        + [pltpu.SemaphoreType.DMA((4 * STEPS,))],
        compiler_params=params(),
        cost_estimate=pl.CostEstimate(flops=ROWS * COLS, bytes_accessed=6 * ROWS * COLS, transcendentals=0),
    )(c, *in_hbm(gradient, error))


def pair_kernel(own_ref, *refs):
    chunks, (o_ref, a, b, sem) = refs[:CHUNKS], refs[CHUNKS:]
    cuts = [slice(k * STEP, (k + 1) * STEP) for k in range(STEPS)]
    parts = [slice(k % 2 * STEP, (k % 2 + 1) * STEP) for k in range(STEPS)]
    groups = [[(own_ref.at[:, cuts[k]], a.at[k]), (chunks[k // 2].at[:, parts[k]], b.at[k])] for k in range(STEPS)]
    stream = Stream(groups, sem)
    sends = []
    for k, cut in enumerate(cuts):
        stream.get(k)
        a[k] = (a[k].astype(F32) + b[k].astype(F32)).astype(BF16)
        sends += load([(a.at[k], o_ref.at[:, cut])], sem, 2 * STEPS + k)
    for send in sends:
        send.wait()


def pair(own, chunks):
    return pl.pallas_call(
        pair_kernel,
        in_specs=[HBM] * (1 + CHUNKS),
        out_specs=HBM,
        out_shape=pltpu.HBM((ROWS, HALF), BF16),
        scratch_shapes=[pltpu.VMEM((STEPS, ROWS, STEP), BF16)] * 2 + [pltpu.SemaphoreType.DMA((3 * STEPS,))],
        compiler_params=params(),
        cost_estimate=pl.CostEstimate(flops=ROWS * HALF, bytes_accessed=6 * ROWS * HALF, transcendentals=0),
    )(*in_hbm(own, *chunks))


def project_kernel(c_ref, q_ref, a_ref, keep_ref, give_ref, acc, a, sem):
    cuts = [slice(k * CHUNK, (k + 1) * CHUNK) for k in range(CHUNKS)]
    stream = Stream([[(a_ref.at[:, cut], a.at[:, cut])] for cut in cuts], sem)
    for k, cut in enumerate(cuts):
        stream.get(k)
        x = jnp.dot(a[:, cut], q_ref[cut, :], preferred_element_type=F32)
        acc[...] = x if k == 0 else acc[...] + x
    c, h = c_ref[0], ROWS // 2
    keep_ref[...] = acc[pl.ds(pl.multiple_of(c * h, h), h), :]
    give_ref[...] = acc[pl.ds(pl.multiple_of((1 - c) * h, h), h), :]


def project(c, query, a):
    out = jax.ShapeDtypeStruct((ROWS // 2, RANK), F32)
    return pl.pallas_call(
        project_kernel,
        in_specs=[SMEM, VMEM, HBM],
        out_specs=[VMEM, VMEM],
        out_shape=[out, out],
        scratch_shapes=[
            pltpu.VMEM((ROWS, RANK), F32),
            pltpu.VMEM((ROWS, HALF), BF16),
            pltpu.SemaphoreType.DMA((CHUNKS,)),
        ],
        compiler_params=params(),
        cost_estimate=pl.CostEstimate(flops=2 * ROWS * HALF * RANK, bytes_accessed=2 * ROWS * HALF + 2 * HALF * RANK, transcendentals=0),
    )(c, query, *in_hbm(a))


def gram_kernel(c_ref, mine_ref, theirs_ref, s_ref, st_ref, g_ref):
    c = c_ref[0]
    h = ROWS // 2
    x, y = mine_ref[...], theirs_ref[...]
    s_ref[:h, :] = pick(c, x, y)
    s_ref[h:, :] = pick(c, y, x)
    s = s_ref[...]
    st = s.T
    st_ref[...] = st
    r = RANK // 2
    g_ref[...] = jnp.dot(pick(c, st[:r], st[r:]), s, preferred_element_type=F32).astype(BF16)


def gram_rows(c, mine, theirs):
    return pl.pallas_call(
        gram_kernel,
        grid=(1,),
        in_specs=[SMEM, VMEM, VMEM],
        out_specs=[pl.BlockSpec((ROWS, RANK), lambda j: (0, 0)), VMEM, VMEM],
        out_shape=[
            pltpu.HBM((ROWS, RANK), BF16),
            jax.ShapeDtypeStruct((RANK, ROWS), BF16),
            jax.ShapeDtypeStruct((RANK // 2, RANK), BF16),
        ],
        compiler_params=params(),
        cost_estimate=pl.CostEstimate(flops=2 * ROWS * RANK * RANK, bytes_accessed=4 * ROWS * RANK, transcendentals=0),
    )(c, mine, theirs)


def term_kernel(st_ref, a_ref, t_ref, a, t, sem):
    cuts = [slice(k * CHUNK, (k + 1) * CHUNK) for k in range(CHUNKS)]
    stream = Stream([[(a_ref.at[:, cut], a.at[k])] for k, cut in enumerate(cuts)], sem)
    st = st_ref[...]
    sends = []
    for k in range(CHUNKS):
        stream.get(k)
        x = jnp.dot(st, a[k], preferred_element_type=F32)
        t[k] = x.astype(BF16).reshape(NM, GROUP, CHUNK)
        sends += load([(t.at[k], t_ref.at[k])], sem, CHUNKS + k)
    for send in sends:
        send.wait()


def term(st, a):
    return pl.pallas_call(
        term_kernel,
        in_specs=[VMEM, HBM],
        out_specs=HBM,
        out_shape=pltpu.HBM((NZ, NM, GROUP, CHUNK), BF16),
        scratch_shapes=[
            pltpu.VMEM((CHUNKS, ROWS, CHUNK), BF16),
            pltpu.VMEM((NZ, NM, GROUP, CHUNK), BF16),
            pltpu.SemaphoreType.DMA((2 * CHUNKS,)),
        ],
        compiler_params=params(),
        cost_estimate=pl.CostEstimate(flops=2 * ROWS * HALF * RANK, bytes_accessed=2 * ROWS * HALF + 2 * HALF * RANK, transcendentals=0),
    )(st, *in_hbm(a))


def total_kernel(x_ref, o_ref, copy, sem):
    n, k = x_ref.shape[0], copy.shape[0]
    total = jnp.sum(x_ref[...].astype(F32), axis=0).astype(BF16)
    copy[...] = jnp.broadcast_to(total[None], copy.shape)
    for send in load([(copy, o_ref.at[pl.ds(i, k)]) for i in range(0, n, k)], sem):
        send.wait()


def total(pieces):
    k = 16
    return pl.pallas_call(
        total_kernel,
        in_specs=[VMEM],
        out_specs=HBM,
        out_shape=pltpu.HBM(pieces.shape, BF16),
        scratch_shapes=[
            pltpu.VMEM((k,) + pieces.shape[1:], BF16),
            pltpu.SemaphoreType.DMA((pieces.shape[0] // k,)),
        ],
        compiler_params=params(),
        cost_estimate=pl.CostEstimate(flops=pieces.size, bytes_accessed=4 * pieces.size, transcendentals=0),
    )(pieces)


def dot_hi(a, b, dims=(((1,), (0,)), ((), ()))):
    return lax.dot_general(a, b, dims, precision=lax.Precision.HIGHEST, preferred_element_type=F32)


NT_DOT = (((1,), (1,)), ((), ()))
BASE = 64


def inverse_factor(a):
    n = a.shape[0]
    if n > BASE:
        h = n // 2
        i11 = inverse_factor(a[:h, :h])
        l21 = dot_hi(a[h:, :h], i11, NT_DOT)
        i22 = inverse_factor(a[h:, h:] - dot_hi(l21, l21, NT_DOT))
        i21 = -dot_hi(i22, dot_hi(l21, i11))
        return jnp.concatenate(
            [jnp.concatenate([i11, jnp.zeros((h, h), F32)], axis=1), jnp.concatenate([i21, i22], axis=1)], axis=0
        )
    row = lax.broadcasted_iota(jnp.int32, (n, 2 * n), 0)
    lane = lax.broadcasted_iota(jnp.int32, (n, 2 * n), 1)
    x = jnp.concatenate([a, jnp.where(row == lane, 1.0, 0.0)[:, :n].astype(F32)], axis=1)
    for j in range(n - 1):
        column = jnp.broadcast_to(x[:, j : j + 1], x.shape)
        pivot = column[j : j + 1, :]
        ratio = jnp.where(row > j, column, 0.0) * (1.0 / pivot)
        x = x - ratio * x[j : j + 1, :]
    d = jnp.sum(jnp.where(row == lane, x, 0.0), axis=1, keepdims=True)
    return x[:, n:] * (1.0 / jnp.sqrt(d))


def solve_kernel(g_ref, s_ref, inv_ref, w_ref):
    inv = inverse_factor(g_ref[...])
    inv_ref[...] = inv
    basis = dot_hi(s_ref[...].astype(F32), inv, NT_DOT)
    w_ref[...] = (dot_hi(basis, inv) * 0.125).astype(BF16)


def solve(gram, summed):
    square = pl.BlockSpec((RANK, RANK), lambda j: (0, 0))
    tall = pl.BlockSpec((ROWS, RANK), lambda j: (0, 0))
    return pl.pallas_call(
        solve_kernel,
        grid=(1,),
        in_specs=[VMEM, tall],
        out_specs=[square, tall],
        out_shape=[pltpu.HBM((RANK, RANK), F32), pltpu.HBM((ROWS, RANK), BF16)],
        compiler_params=params(),
        cost_estimate=pl.CostEstimate(flops=2 * 10**10, bytes_accessed=10**6, transcendentals=0),
    )(gram, *in_hbm(summed))


def finish_kernel(held, s_ref, w_ref, inv_ref, t_ref, *refs):
    ins, (err_ref, f_ref, t, a, out, f, w_in, inv_in, sem) = refs[:-9], refs[-9:]
    core, m = s_ref[0], s_ref[1]
    t = t_ref if held else t
    if ins[0].shape[1] == HALF:
        parts = [ins[0].at[:, k * CHUNK : (k + 1) * CHUNK] for k in range(CHUNKS)]
    else:
        parts = ins[:CHUNKS]
    first = load([(w_ref, w_in)], sem)
    groups = [[(parts[k], a.at[k])] for k in range(CHUNKS)]
    if t is not t_ref:
        groups = [[(t_ref.at[k], t.at[k])] + group for k, group in enumerate(groups)]
    stream = Stream(groups, sem.at[pl.ds(2, 2 * CHUNKS)])
    first += load([(inv_ref, inv_in)], sem, 1)
    first[0].wait()
    w = w_in[...]
    sends, at = [], 2 + 2 * CHUNKS
    for k in range(CHUNKS):
        stream.get(k)
        x = jnp.dot(w, t[k].reshape(RANK, CHUNK), preferred_element_type=F32)
        out[k] = (a[k].astype(F32) - x).astype(BF16)
        for s in range(CHUNK // SUB):
            to = pl.ds(pl.multiple_of((k * (CHUNK // SUB) + s) * BLK + core * SUB, SUB), SUB)
            sends += load([(out.at[k, :, s * SUB : (s + 1) * SUB], err_ref.at[:, to])], sem, at + len(sends))
    first[1].wait()
    per = CHUNK // SUB
    x = t[m // per, :, :, pl.ds(pl.multiple_of(m % per * SUB, SUB), SUB)].reshape(RANK, SUB)
    f[...] = dot_hi(inv_in[...], x.astype(F32)).T * 0.125
    sends += load([(f, f_ref.at[pl.ds(pl.multiple_of(core * SUB, SUB), SUB)])], sem, at + len(sends))
    for send in sends:
        send.wait()


def finish(held, where, w, inv, t, parts, before=()):
    n = 4 + len(parts)
    return pl.pallas_call(
        functools.partial(finish_kernel, held),
        in_specs=[SMEM, HBM, HBM, VMEM if held else HBM] + [HBM] * (len(parts) + len(before)),
        out_specs=[HBM, HBM],
        out_shape=[pltpu.HBM((ROWS, COLS), BF16), pltpu.HBM((BLK, RANK), F32)],
        input_output_aliases={n + i: i for i in range(len(before))},
        scratch_shapes=[
            pltpu.VMEM((1 if held else NZ, NM, GROUP, CHUNK), BF16),
            pltpu.VMEM((CHUNKS, ROWS, CHUNK), BF16),
            pltpu.VMEM((CHUNKS, ROWS, CHUNK), BF16),
            pltpu.VMEM((SUB, RANK), F32),
            pltpu.VMEM((ROWS, RANK), BF16),
            pltpu.VMEM((RANK, RANK), F32),
            pltpu.SemaphoreType.DMA((3 + 2 * CHUNKS + NM,)),
        ],
        compiler_params=params(),
        cost_estimate=pl.CostEstimate(flops=2 * ROWS * HALF * RANK, bytes_accessed=4 * ROWS * HALF + 2 * HALF * RANK, transcendentals=0),
    )(where, *in_hbm(w, inv), t if held else in_hbm(t)[0], *in_hbm(*parts, *before))


def swap(x):
    return lax.ppermute(x, "c", [(0, 1), (1, 0)])


def ring_sum(x, axis):
    x1, x2, x3 = (lax.ppermute(x, axis, [(i, (i + k) % 4) for i in range(4)]) for k in (1, 2, 3))
    return (x.astype(F32) + x2.astype(F32)) + (x1.astype(F32) + x3.astype(F32))


def join(c, mine, theirs):
    return jnp.concatenate([pick(c, mine, theirs), pick(c, theirs, mine)], axis=0)


def shards(gradient, error, query):
    gradient, error = gradient[0], error[0]
    c = lax.axis_index("c").astype(jnp.int32)
    m = (lax.axis_index("x") * 4 + lax.axis_index("y")).astype(jnp.int32)
    cv = c.reshape(1)

    with jax.named_scope("query_gather"):
        part = lax.dynamic_slice_in_dim(query, c * SUB, SUB, 0)
        copies = jnp.broadcast_to(part[None], (NM, SUB, RANK))
        half_query = lax.all_to_all(copies, ("x", "y"), 0, 0, tiled=True).reshape(HALF, RANK)

    with jax.named_scope("adjust"):
        own, *others = adjust(cv, gradient, error)
        both = pair(own, [swap(other) for other in others])

    with jax.named_scope("project"):
        keep, give = project(cv, half_query, both)
        chip = (keep + swap(give)).astype(BF16)
        rows = ring_sum(chip, "z").astype(BF16)

    with jax.named_scope("gram"):
        summed, summed_t, gram_x = gram_rows(cv, rows, swap(rows))
        gram_x = ring_sum(gram_x, "x")

    with jax.named_scope("term"):
        pieces = term(summed_t, both).reshape(NZ * NM, RANK // NM, HALF // NZ)
        pieces, gram_x = lax.optimization_barrier((pieces, gram_x))
        pieces = lax.all_to_all(pieces, ("z", "x", "y"), 0, 0, tiled=True)

    with jax.named_scope("gather"):
        gram_y = ring_sum(gram_x, "y")
        sums, gram_y = lax.optimization_barrier((total(pieces), gram_y))
        mine = lax.all_to_all(sums, ("z", "x", "y"), 0, 0, tiled=True)

    with jax.named_scope("solve"):
        inv, w = solve(join(c, gram_y, swap(gram_y)), summed)
        mine, inv, w = lax.optimization_barrier((mine, inv, w))

    with jax.named_scope("finish"):
        mine = mine.reshape(NZ, NM, GROUP, CHUNK)
        theirs = swap(mine)
        out = finish(True, jnp.stack([c, m]), w, inv, mine, [own])
        new_error, factor = finish(False, jnp.stack([1 - c, m]), w, inv, theirs, others, out)
    return factor, new_error[None]


def solution(mesh):
    grid = Mesh(mesh.devices.reshape(4, 2, 4, 4), ("z", "c", "x", "y"))
    in_specs = (P(("z", "c"), ("x", "y"), None), P(("z", "c"), ("x", "y"), None), P(("x", "y"), None))
    out_specs = (P(("x", "y"), None), P(("z", "c"), ("x", "y"), None))
    return jax.shard_map(shards, mesh=grid, in_specs=in_specs, out_specs=out_specs, check_vma=False)
```

```python
import functools

import jax
import jax.numpy as jnp
from jax import lax
from jax.experimental import pallas as pl
from jax.experimental.pallas import tpu as pltpu
from jax.sharding import Mesh, PartitionSpec as P

BF16 = jnp.bfloat16
F32 = jnp.float32
VMEM_LIMIT = 40 * 1024 * 1024
ROWS, COLS, RANK = 512, 8192, 256
NZ, NM = 4, 16
HALF = COLS // 2
BLK = COLS // NM
SUB = BLK // 2
TN_DOT = (((0,), (0,)), ((), ()))

SMEM = pl.BlockSpec(memory_space=pltpu.SMEM)
VMEM = pl.BlockSpec(memory_space=pltpu.VMEM)
HBM = pl.BlockSpec(memory_space=pltpu.HBM)
CHUNKS = 4
CHUNK = HALF // CHUNKS
STEP = CHUNK // 2
STEPS = HALF // STEP
GROUP = RANK // NM


def params(limit=VMEM_LIMIT):
    return pltpu.CompilerParams(vmem_limit_bytes=limit)


def in_hbm(*arrays):
    return [pltpu.with_memory_space_constraint(x, pltpu.HBM) for x in arrays]


def load(pairs, sem, first=0):
    copies = [pltpu.make_async_copy(src, dst, sem.at[first + i]) for i, (src, dst) in enumerate(pairs)]
    for copy in copies:
        copy.start()
    return copies


class Stream:
    DEPTH = 4

    def __init__(self, groups, sem):
        self.groups, self.sem, self.started = groups, sem, []
        for _ in range(self.DEPTH):
            self.more()

    def more(self):
        k = len(self.started)
        if k < len(self.groups):
            self.started.append(load(self.groups[k], self.sem, sum(len(g) for g in self.groups[:k])))

    def get(self, k):
        for copy in self.started[k]:
            copy.wait()
        self.more()


def pick(c, first, second):
    return jnp.where(c == 0, first, second)


def adjust_kernel(c_ref, g_ref, d_ref, own_ref, *refs):
    chunks, (g, d, own, other, sem) = refs[:CHUNKS], refs[CHUNKS:]
    wide = [slice(2 * k * STEP, 2 * (k + 1) * STEP) for k in range(STEPS)]
    stream = Stream([[(g_ref.at[:, cut], g.at[k]), (d_ref.at[:, cut], d.at[k])] for k, cut in enumerate(wide)], sem)
    c = c_ref[0]
    sends = []
    for k in range(STEPS):
        stream.get(k)
        for s in range(STEP // SUB):
            part = slice(s * SUB, (s + 1) * SUB)
            for out, core in ((own, c), (other, 1 - c)):
                cut = pl.ds(pl.multiple_of(s * BLK + core * SUB, SUB), SUB)
                out[k, :, part] = (g[k, :, cut].astype(F32) + d[k, :, cut].astype(F32)).astype(BF16)
        cut = slice(k * STEP, (k + 1) * STEP)
        part = slice(k % 2 * STEP, (k % 2 + 1) * STEP)
        pairs = [(own.at[k], own_ref.at[:, cut]), (other.at[k], chunks[k // 2].at[:, part])]
        sends += load(pairs, sem, 2 * STEPS + 2 * k)
    for send in sends:
        send.wait()


def adjust(c, gradient, error):
    return pl.pallas_call(
        adjust_kernel,
        in_specs=[SMEM, HBM, HBM],
        out_specs=[HBM] * (1 + CHUNKS),
        out_shape=[pltpu.HBM((ROWS, HALF), BF16)] + [pltpu.HBM((ROWS, CHUNK), BF16)] * CHUNKS,
        scratch_shapes=[pltpu.VMEM((STEPS, ROWS, 2 * STEP), BF16)] * 2
        + [pltpu.VMEM((STEPS, ROWS, STEP), BF16)] * 2
        + [pltpu.SemaphoreType.DMA((4 * STEPS,))],
        compiler_params=params(),
        cost_estimate=pl.CostEstimate(flops=ROWS * COLS, bytes_accessed=6 * ROWS * COLS, transcendentals=0),
    )(c, *in_hbm(gradient, error))


def pair_kernel(own_ref, *refs):
    chunks, (o_ref, a, b, sem) = refs[:CHUNKS], refs[CHUNKS:]
    cuts = [slice(k * STEP, (k + 1) * STEP) for k in range(STEPS)]
    parts = [slice(k % 2 * STEP, (k % 2 + 1) * STEP) for k in range(STEPS)]
    groups = [[(own_ref.at[:, cuts[k]], a.at[k]), (chunks[k // 2].at[:, parts[k]], b.at[k])] for k in range(STEPS)]
    stream = Stream(groups, sem)
    sends = []
    for k, cut in enumerate(cuts):
        stream.get(k)
        a[k] = (a[k].astype(F32) + b[k].astype(F32)).astype(BF16)
        sends += load([(a.at[k], o_ref.at[:, cut])], sem, 2 * STEPS + k)
    for send in sends:
        send.wait()


def pair(own, chunks):
    return pl.pallas_call(
        pair_kernel,
        in_specs=[HBM] * (1 + CHUNKS),
        out_specs=HBM,
        out_shape=pltpu.HBM((ROWS, HALF), BF16),
        scratch_shapes=[pltpu.VMEM((STEPS, ROWS, STEP), BF16)] * 2 + [pltpu.SemaphoreType.DMA((3 * STEPS,))],
        compiler_params=params(),
        cost_estimate=pl.CostEstimate(flops=ROWS * HALF, bytes_accessed=6 * ROWS * HALF, transcendentals=0),
    )(*in_hbm(own, *chunks))


def project_kernel(c_ref, q_ref, a_ref, keep_ref, give_ref, acc, a, sem):
    cuts = [slice(k * CHUNK, (k + 1) * CHUNK) for k in range(CHUNKS)]
    stream = Stream([[(a_ref.at[:, cut], a.at[:, cut])] for cut in cuts], sem)
    for k, cut in enumerate(cuts):
        stream.get(k)
        x = jnp.dot(a[:, cut], q_ref[cut, :], preferred_element_type=F32)
        acc[...] = x if k == 0 else acc[...] + x
    c, h = c_ref[0], ROWS // 2
    keep_ref[...] = acc[pl.ds(pl.multiple_of(c * h, h), h), :]
    give_ref[...] = acc[pl.ds(pl.multiple_of((1 - c) * h, h), h), :]


def project(c, query, a):
    out = jax.ShapeDtypeStruct((ROWS // 2, RANK), F32)
    return pl.pallas_call(
        project_kernel,
        in_specs=[SMEM, VMEM, HBM],
        out_specs=[VMEM, VMEM],
        out_shape=[out, out],
        scratch_shapes=[
            pltpu.VMEM((ROWS, RANK), F32),
            pltpu.VMEM((ROWS, HALF), BF16),
            pltpu.SemaphoreType.DMA((CHUNKS,)),
        ],
        compiler_params=params(),
        cost_estimate=pl.CostEstimate(flops=2 * ROWS * HALF * RANK, bytes_accessed=2 * ROWS * HALF + 2 * HALF * RANK, transcendentals=0),
    )(c, query, *in_hbm(a))


def gram_kernel(c_ref, mine_ref, theirs_ref, s_ref, st_ref, g_ref):
    c = c_ref[0]
    h = ROWS // 2
    x, y = mine_ref[...], theirs_ref[...]
    s_ref[:h, :] = pick(c, x, y)
    s_ref[h:, :] = pick(c, y, x)
    s = s_ref[...]
    st = s.T
    st_ref[...] = st
    r = RANK // 2
    g_ref[...] = jnp.dot(pick(c, st[:r], st[r:]), s, preferred_element_type=F32).astype(BF16)


def gram_rows(c, mine, theirs):
    return pl.pallas_call(
        gram_kernel,
        grid=(1,),
        in_specs=[SMEM, VMEM, VMEM],
        out_specs=[pl.BlockSpec((ROWS, RANK), lambda j: (0, 0)), VMEM, VMEM],
        out_shape=[
            pltpu.HBM((ROWS, RANK), BF16),
            jax.ShapeDtypeStruct((RANK, ROWS), BF16),
            jax.ShapeDtypeStruct((RANK // 2, RANK), BF16),
        ],
        compiler_params=params(),
        cost_estimate=pl.CostEstimate(flops=2 * ROWS * RANK * RANK, bytes_accessed=4 * ROWS * RANK, transcendentals=0),
    )(c, mine, theirs)


def term_kernel(st_ref, a_ref, t_ref, a, t, sem):
    cuts = [slice(k * CHUNK, (k + 1) * CHUNK) for k in range(CHUNKS)]
    stream = Stream([[(a_ref.at[:, cut], a.at[k])] for k, cut in enumerate(cuts)], sem)
    st = st_ref[...]
    sends = []
    for k in range(CHUNKS):
        stream.get(k)
        x = jnp.dot(st, a[k], preferred_element_type=F32)
        t[k] = x.astype(BF16).reshape(NM, GROUP, CHUNK)
        sends += load([(t.at[k], t_ref.at[k])], sem, CHUNKS + k)
    for send in sends:
        send.wait()


def term(st, a):
    return pl.pallas_call(
        term_kernel,
        in_specs=[VMEM, HBM],
        out_specs=HBM,
        out_shape=pltpu.HBM((NZ, NM, GROUP, CHUNK), BF16),
        scratch_shapes=[
            pltpu.VMEM((CHUNKS, ROWS, CHUNK), BF16),
            pltpu.VMEM((NZ, NM, GROUP, CHUNK), BF16),
            pltpu.SemaphoreType.DMA((2 * CHUNKS,)),
        ],
        compiler_params=params(),
        cost_estimate=pl.CostEstimate(flops=2 * ROWS * HALF * RANK, bytes_accessed=2 * ROWS * HALF + 2 * HALF * RANK, transcendentals=0),
    )(st, *in_hbm(a))


def total_kernel(x_ref, o_ref, copy, sem):
    n, k = x_ref.shape[0], copy.shape[0]
    total = jnp.sum(x_ref[...].astype(F32), axis=0).astype(BF16)
    copy[...] = jnp.broadcast_to(total[None], copy.shape)
    for send in load([(copy, o_ref.at[pl.ds(i, k)]) for i in range(0, n, k)], sem):
        send.wait()


def total(pieces):
    k = 16
    return pl.pallas_call(
        total_kernel,
        in_specs=[VMEM],
        out_specs=HBM,
        out_shape=pltpu.HBM(pieces.shape, BF16),
        scratch_shapes=[
            pltpu.VMEM((k,) + pieces.shape[1:], BF16),
            pltpu.SemaphoreType.DMA((pieces.shape[0] // k,)),
        ],
        compiler_params=params(),
        cost_estimate=pl.CostEstimate(flops=pieces.size, bytes_accessed=4 * pieces.size, transcendentals=0),
    )(pieces)


def dot_hi(a, b, dims=(((1,), (0,)), ((), ()))):
    return lax.dot_general(a, b, dims, precision=lax.Precision.HIGHEST, preferred_element_type=F32)


NT_DOT = (((1,), (1,)), ((), ()))
BASE = 64
PANEL = 16


def inverse_factor(a):
    n = a.shape[0]
    if n > BASE:
        h = n // 2
        i11 = inverse_factor(a[:h, :h])
        l21 = dot_hi(a[h:, :h], i11, NT_DOT)
        i22 = inverse_factor(a[h:, h:] - dot_hi(l21, l21, NT_DOT))
        i21 = -dot_hi(i22, dot_hi(l21, i11))
        return jnp.concatenate(
            [jnp.concatenate([i11, jnp.zeros((h, h), F32)], axis=1), jnp.concatenate([i21, i22], axis=1)], axis=0
        )
    row = lax.broadcasted_iota(jnp.int32, (n, 2 * n), 0)
    lane = lax.broadcasted_iota(jnp.int32, (n, 2 * n), 1)
    x = jnp.concatenate([a, jnp.where(row == lane, 1.0, 0.0)[:, :n].astype(F32)], axis=1)
    for first in range(0, n, PANEL):
        columns = [jnp.broadcast_to(x[:, j : j + 1], x.shape) for j in range(first, first + PANEL)]
        for i in range(min(PANEL, n - 1 - first)):
            j = first + i
            ratio = jnp.where(row > j, columns[i], 0.0) * (1.0 / columns[i][j : j + 1, :])
            for k in range(i + 1, PANEL):
                columns[k] = columns[k] - ratio * columns[k][j : j + 1, :]
            x = x - ratio * x[j : j + 1, :]
    d = jnp.sum(jnp.where(row == lane, x, 0.0), axis=1, keepdims=True)
    return x[:, n:] * (1.0 / jnp.sqrt(d))


def solve_kernel(g_ref, s_ref, inv_ref, w_ref):
    inv = inverse_factor(g_ref[...])
    inv_ref[...] = inv
    basis = dot_hi(s_ref[...].astype(F32), inv, NT_DOT)
    w_ref[...] = (dot_hi(basis, inv) * 0.125).astype(BF16)


def solve(gram, summed):
    square = pl.BlockSpec((RANK, RANK), lambda j: (0, 0))
    tall = pl.BlockSpec((ROWS, RANK), lambda j: (0, 0))
    return pl.pallas_call(
        solve_kernel,
        grid=(1,),
        in_specs=[VMEM, tall],
        out_specs=[square, tall],
        out_shape=[pltpu.HBM((RANK, RANK), F32), pltpu.HBM((ROWS, RANK), BF16)],
        compiler_params=params(),
        cost_estimate=pl.CostEstimate(flops=2 * 10**10, bytes_accessed=10**6, transcendentals=0),
    )(gram, *in_hbm(summed))


def finish_kernel(held, s_ref, w_ref, inv_ref, t_ref, *refs):
    ins, (err_ref, f_ref, t, a, out, f, w_in, inv_in, sem) = refs[:-9], refs[-9:]
    core, m = s_ref[0], s_ref[1]
    t = t_ref if held else t
    if ins[0].shape[1] == HALF:
        parts = [ins[0].at[:, k * CHUNK : (k + 1) * CHUNK] for k in range(CHUNKS)]
    else:
        parts = ins[:CHUNKS]
    first = load([(w_ref, w_in)], sem)
    groups = [[(parts[k], a.at[k])] for k in range(CHUNKS)]
    if t is not t_ref:
        groups = [[(t_ref.at[k], t.at[k])] + group for k, group in enumerate(groups)]
    stream = Stream(groups, sem.at[pl.ds(2, 2 * CHUNKS)])
    first += load([(inv_ref, inv_in)], sem, 1)
    first[0].wait()
    w = w_in[...]
    sends, at = [], 2 + 2 * CHUNKS
    for k in range(CHUNKS):
        stream.get(k)
        x = jnp.dot(w, t[k].reshape(RANK, CHUNK), preferred_element_type=F32)
        out[k] = (a[k].astype(F32) - x).astype(BF16)
        for s in range(CHUNK // SUB):
            to = pl.ds(pl.multiple_of((k * (CHUNK // SUB) + s) * BLK + core * SUB, SUB), SUB)
            sends += load([(out.at[k, :, s * SUB : (s + 1) * SUB], err_ref.at[:, to])], sem, at + len(sends))
    first[1].wait()
    per = CHUNK // SUB
    x = t[m // per, :, :, pl.ds(pl.multiple_of(m % per * SUB, SUB), SUB)].reshape(RANK, SUB)
    f[...] = dot_hi(inv_in[...], x.astype(F32)).T * 0.125
    sends += load([(f, f_ref.at[pl.ds(pl.multiple_of(core * SUB, SUB), SUB)])], sem, at + len(sends))
    for send in sends:
        send.wait()


def finish(held, where, w, inv, t, parts, before=()):
    n = 4 + len(parts)
    return pl.pallas_call(
        functools.partial(finish_kernel, held),
        in_specs=[SMEM, HBM, HBM, VMEM if held else HBM] + [HBM] * (len(parts) + len(before)),
        out_specs=[HBM, HBM],
        out_shape=[pltpu.HBM((ROWS, COLS), BF16), pltpu.HBM((BLK, RANK), F32)],
        input_output_aliases={n + i: i for i in range(len(before))},
        scratch_shapes=[
            pltpu.VMEM((1 if held else NZ, NM, GROUP, CHUNK), BF16),
            pltpu.VMEM((CHUNKS, ROWS, CHUNK), BF16),
            pltpu.VMEM((CHUNKS, ROWS, CHUNK), BF16),
            pltpu.VMEM((SUB, RANK), F32),
            pltpu.VMEM((ROWS, RANK), BF16),
            pltpu.VMEM((RANK, RANK), F32),
            pltpu.SemaphoreType.DMA((3 + 2 * CHUNKS + NM,)),
        ],
        compiler_params=params(),
        cost_estimate=pl.CostEstimate(flops=2 * ROWS * HALF * RANK, bytes_accessed=4 * ROWS * HALF + 2 * HALF * RANK, transcendentals=0),
    )(where, *in_hbm(w, inv), t if held else in_hbm(t)[0], *in_hbm(*parts, *before))


def swap(x):
    return lax.ppermute(x, "c", [(0, 1), (1, 0)])


def ring_sum(x, axis):
    x1, x3, x2 = (lax.ppermute(x, axis, [(i, (i + k) % 4) for i in range(4)]) for k in (1, 3, 2))
    return (x.astype(F32) + x2.astype(F32)) + (x1.astype(F32) + x3.astype(F32))


def join(c, mine, theirs):
    return jnp.concatenate([pick(c, mine, theirs), pick(c, theirs, mine)], axis=0)


def shards(gradient, error, query):
    gradient, error = gradient[0], error[0]
    c = lax.axis_index("c").astype(jnp.int32)
    m = (lax.axis_index("x") * 4 + lax.axis_index("y")).astype(jnp.int32)
    cv = c.reshape(1)

    with jax.named_scope("query_gather"):
        part = lax.dynamic_slice_in_dim(query, c * SUB, SUB, 0)
        copies = jnp.broadcast_to(part[None], (NM, SUB, RANK))
        half_query = lax.all_to_all(copies, ("x", "y"), 0, 0, tiled=True).reshape(HALF, RANK)

    with jax.named_scope("adjust"):
        own, *others = adjust(cv, gradient, error)
        both = pair(own, [swap(other) for other in others])

    with jax.named_scope("project"):
        keep, give = project(cv, half_query, both)
        chip = (keep + swap(give)).astype(BF16)
        rows = ring_sum(chip, "z").astype(BF16)

    with jax.named_scope("gram"):
        summed, summed_t, gram_x = gram_rows(cv, rows, swap(rows))
        gram_x = ring_sum(gram_x, "x")

    with jax.named_scope("term"):
        pieces = term(summed_t, both).reshape(NZ * NM, RANK // NM, HALF // NZ)
        pieces, gram_x = lax.optimization_barrier((pieces, gram_x))
        pieces = lax.all_to_all(pieces, ("z", "x", "y"), 0, 0, tiled=True)

    with jax.named_scope("gather"):
        gram_y = ring_sum(gram_x.astype(BF16), "y")
        sums, gram_y = lax.optimization_barrier((total(pieces), gram_y))
        mine = lax.all_to_all(sums, ("z", "x", "y"), 0, 0, tiled=True)

    with jax.named_scope("solve"):
        inv, w = solve(join(c, gram_y, swap(gram_y)), summed)
        mine, inv, w = lax.optimization_barrier((mine, inv, w))

    with jax.named_scope("finish"):
        mine = mine.reshape(NZ, NM, GROUP, CHUNK)
        theirs = swap(mine)
        out = finish(True, jnp.stack([c, m]), w, inv, mine, [own])
        new_error, factor = finish(False, jnp.stack([1 - c, m]), w, inv, theirs, others, out)
    return factor, new_error[None]


def solution(mesh):
    grid = Mesh(mesh.devices.reshape(4, 2, 4, 4), ("z", "c", "x", "y"))
    in_specs = (P(("z", "c"), ("x", "y"), None), P(("z", "c"), ("x", "y"), None), P(("x", "y"), None))
    out_specs = (P(("x", "y"), None), P(("z", "c"), ("x", "y"), None))
    return jax.shard_map(shards, mesh=grid, in_specs=in_specs, out_specs=out_specs, check_vma=False)
```

```python
import functools

import jax
import jax.numpy as jnp
from jax import lax
from jax.experimental import pallas as pl
from jax.experimental.pallas import tpu as pltpu
from jax.sharding import Mesh, PartitionSpec as P

BF16 = jnp.bfloat16
F32 = jnp.float32
VMEM_LIMIT = 40 * 1024 * 1024
ROWS, COLS, RANK = 512, 8192, 256
NZ, NM = 4, 16
HALF = COLS // 2
BLK = COLS // NM
SUB = BLK // 2
TN_DOT = (((0,), (0,)), ((), ()))

SMEM = pl.BlockSpec(memory_space=pltpu.SMEM)
VMEM = pl.BlockSpec(memory_space=pltpu.VMEM)
HBM = pl.BlockSpec(memory_space=pltpu.HBM)
CHUNKS = 4
CHUNK = HALF // CHUNKS
STEP = CHUNK // 2
STEPS = HALF // STEP
GROUP = RANK // NM


def params(limit=VMEM_LIMIT):
    return pltpu.CompilerParams(vmem_limit_bytes=limit)


def in_hbm(*arrays):
    return [pltpu.with_memory_space_constraint(x, pltpu.HBM) for x in arrays]


def load(pairs, sem, first=0):
    copies = [pltpu.make_async_copy(src, dst, sem.at[first + i]) for i, (src, dst) in enumerate(pairs)]
    for copy in copies:
        copy.start()
    return copies


def arrived(dst, sem):
    pltpu.make_async_copy(dst, dst, sem).wait()


def rolled(count, step):
    def body(k, carry):
        step(k)
        return carry

    lax.fori_loop(0, count, body, 0)


def aligned(start, size):
    return pl.ds(pl.multiple_of(start, size), size)


def pick(c, first, second):
    return jnp.where(c == 0, first, second)


def adjust_kernel(c_ref, g_ref, d_ref, own_ref, *refs):
    chunks, (g, d, own, other, sem) = refs[:CHUNKS], refs[CHUNKS:]
    for k in range(STEPS):
        cut = slice(2 * k * STEP, 2 * (k + 1) * STEP)
        load([(g_ref.at[:, cut], g.at[k]), (d_ref.at[:, cut], d.at[k])], sem, 2 * k)
    c = c_ref[0]

    def step(k):
        arrived(g.at[k], sem.at[2 * k])
        arrived(d.at[k], sem.at[2 * k + 1])
        for s in range(STEP // SUB):
            part = slice(s * SUB, (s + 1) * SUB)
            for out, core in ((own, c), (other, 1 - c)):
                cut = aligned(s * BLK + core * SUB, SUB)
                out[k, :, part] = (g[k, :, cut].astype(F32) + d[k, :, cut].astype(F32)).astype(BF16)
        load([(own.at[k], own_ref.at[:, aligned(k * STEP, STEP)])], sem, 2 * STEPS + k)
        for i, ref in enumerate(chunks):

            @pl.when(k // 2 == i)
            def _():
                load([(other.at[k], ref.at[:, aligned(k % 2 * STEP, STEP)])], sem, 3 * STEPS + k)

    rolled(STEPS, step)

    def sent(k):
        arrived(own.at[k], sem.at[2 * STEPS + k])
        arrived(other.at[k], sem.at[3 * STEPS + k])

    rolled(STEPS, sent)


def adjust(c, gradient, error):
    return pl.pallas_call(
        adjust_kernel,
        in_specs=[SMEM, HBM, HBM],
        out_specs=[HBM] * (1 + CHUNKS),
        out_shape=[pltpu.HBM((ROWS, HALF), BF16)] + [pltpu.HBM((ROWS, CHUNK), BF16)] * CHUNKS,
        scratch_shapes=[pltpu.VMEM((STEPS, ROWS, 2 * STEP), BF16)] * 2
        + [pltpu.VMEM((STEPS, ROWS, STEP), BF16)] * 2
        + [pltpu.SemaphoreType.DMA((4 * STEPS,))],
        compiler_params=params(),
        cost_estimate=pl.CostEstimate(flops=ROWS * COLS, bytes_accessed=6 * ROWS * COLS, transcendentals=0),
    )(c, *in_hbm(gradient, error))


def pair_kernel(own_ref, *refs):
    chunks, (o_ref, a, b, sem) = refs[:CHUNKS], refs[CHUNKS:]
    for k in range(STEPS):
        part = slice(k % 2 * STEP, (k % 2 + 1) * STEP)
        load([(own_ref.at[:, k * STEP : (k + 1) * STEP], a.at[k]), (chunks[k // 2].at[:, part], b.at[k])], sem, 2 * k)

    def step(k):
        arrived(a.at[k], sem.at[2 * k])
        arrived(b.at[k], sem.at[2 * k + 1])
        a[k] = (a[k].astype(F32) + b[k].astype(F32)).astype(BF16)
        load([(a.at[k], o_ref.at[:, aligned(k * STEP, STEP)])], sem, 2 * STEPS + k)

    rolled(STEPS, step)
    rolled(STEPS, lambda k: arrived(a.at[k], sem.at[2 * STEPS + k]))


def pair(own, chunks):
    return pl.pallas_call(
        pair_kernel,
        in_specs=[HBM] * (1 + CHUNKS),
        out_specs=HBM,
        out_shape=pltpu.HBM((ROWS, HALF), BF16),
        scratch_shapes=[pltpu.VMEM((STEPS, ROWS, STEP), BF16)] * 2 + [pltpu.SemaphoreType.DMA((3 * STEPS,))],
        compiler_params=params(),
        cost_estimate=pl.CostEstimate(flops=ROWS * HALF, bytes_accessed=6 * ROWS * HALF, transcendentals=0),
    )(*in_hbm(own, *chunks))


def project_kernel(c_ref, q_ref, a_ref, keep_ref, give_ref, acc, a, sem):
    for k in range(CHUNKS):
        load([(a_ref.at[:, k * CHUNK : (k + 1) * CHUNK], a.at[k])], sem, k)
    acc[...] = jnp.zeros_like(acc)

    def step(k):
        arrived(a.at[k], sem.at[k])
        acc[...] += jnp.dot(a[k], q_ref[aligned(k * CHUNK, CHUNK), :], preferred_element_type=F32)

    rolled(CHUNKS, step)
    c, h = c_ref[0], ROWS // 2
    keep_ref[...] = acc[aligned(c * h, h), :]
    give_ref[...] = acc[aligned((1 - c) * h, h), :]


def project(c, query, a):
    out = jax.ShapeDtypeStruct((ROWS // 2, RANK), F32)
    return pl.pallas_call(
        project_kernel,
        in_specs=[SMEM, VMEM, HBM],
        out_specs=[VMEM, VMEM],
        out_shape=[out, out],
        scratch_shapes=[
            pltpu.VMEM((ROWS, RANK), F32),
            pltpu.VMEM((CHUNKS, ROWS, CHUNK), BF16),
            pltpu.SemaphoreType.DMA((CHUNKS,)),
        ],
        compiler_params=params(),
        cost_estimate=pl.CostEstimate(flops=2 * ROWS * HALF * RANK, bytes_accessed=2 * ROWS * HALF + 2 * HALF * RANK, transcendentals=0),
    )(c, query, *in_hbm(a))


def gram_kernel(c_ref, mine_ref, theirs_ref, s_ref, st_ref, g_ref):
    c = c_ref[0]
    h = ROWS // 2
    x, y = mine_ref[...], theirs_ref[...]
    s_ref[:h, :] = pick(c, x, y)
    s_ref[h:, :] = pick(c, y, x)
    s = s_ref[...]
    st = s.T
    st_ref[...] = st
    r = RANK // 2
    g_ref[...] = jnp.dot(pick(c, st[:r], st[r:]), s, preferred_element_type=F32).astype(BF16)


def gram_rows(c, mine, theirs):
    return pl.pallas_call(
        gram_kernel,
        grid=(1,),
        in_specs=[SMEM, VMEM, VMEM],
        out_specs=[pl.BlockSpec((ROWS, RANK), lambda j: (0, 0)), VMEM, VMEM],
        out_shape=[
            pltpu.HBM((ROWS, RANK), BF16),
            jax.ShapeDtypeStruct((RANK, ROWS), BF16),
            jax.ShapeDtypeStruct((RANK // 2, RANK), BF16),
        ],
        compiler_params=params(),
        cost_estimate=pl.CostEstimate(flops=2 * ROWS * RANK * RANK, bytes_accessed=4 * ROWS * RANK, transcendentals=0),
    )(c, mine, theirs)


def term_kernel(st_ref, a_ref, t_ref, a, t, sem):
    for k in range(CHUNKS):
        load([(a_ref.at[:, k * CHUNK : (k + 1) * CHUNK], a.at[k])], sem, k)

    def step(k):
        arrived(a.at[k], sem.at[k])
        x = jnp.dot(st_ref[...], a[k], preferred_element_type=F32)
        t[k] = x.astype(BF16).reshape(NM, GROUP, CHUNK)
        load([(t.at[k], t_ref.at[k])], sem, CHUNKS + k)

    rolled(CHUNKS, step)
    rolled(CHUNKS, lambda k: arrived(t.at[k], sem.at[CHUNKS + k]))


def term(st, a):
    return pl.pallas_call(
        term_kernel,
        in_specs=[VMEM, HBM],
        out_specs=HBM,
        out_shape=pltpu.HBM((NZ, NM, GROUP, CHUNK), BF16),
        scratch_shapes=[
            pltpu.VMEM((CHUNKS, ROWS, CHUNK), BF16),
            pltpu.VMEM((NZ, NM, GROUP, CHUNK), BF16),
            pltpu.SemaphoreType.DMA((2 * CHUNKS,)),
        ],
        compiler_params=params(),
        cost_estimate=pl.CostEstimate(flops=2 * ROWS * HALF * RANK, bytes_accessed=2 * ROWS * HALF + 2 * HALF * RANK, transcendentals=0),
    )(st, *in_hbm(a))


def total_kernel(x_ref, o_ref, copy, sem):
    n, k = x_ref.shape[0], copy.shape[0]
    total = jnp.sum(x_ref[...].astype(F32), axis=0).astype(BF16)
    copy[...] = jnp.broadcast_to(total[None], copy.shape)
    for send in load([(copy, o_ref.at[pl.ds(i, k)]) for i in range(0, n, k)], sem):
        send.wait()


def total(pieces):
    k = 16
    return pl.pallas_call(
        total_kernel,
        in_specs=[VMEM],
        out_specs=HBM,
        out_shape=pltpu.HBM(pieces.shape, BF16),
        scratch_shapes=[
            pltpu.VMEM((k,) + pieces.shape[1:], BF16),
            pltpu.SemaphoreType.DMA((pieces.shape[0] // k,)),
        ],
        compiler_params=params(),
        cost_estimate=pl.CostEstimate(flops=pieces.size, bytes_accessed=4 * pieces.size, transcendentals=0),
    )(pieces)


def dot_hi(a, b, dims=(((1,), (0,)), ((), ()))):
    return lax.dot_general(a, b, dims, precision=lax.Precision.HIGHEST, preferred_element_type=F32)


NT_DOT = (((1,), (1,)), ((), ()))
BASE = 64
PANEL = 16


def inverse_factor(a):
    n = a.shape[0]
    if n > BASE:
        h = n // 2
        i11 = inverse_factor(a[:h, :h])
        l21 = dot_hi(a[h:, :h], i11, NT_DOT)
        i22 = inverse_factor(a[h:, h:] - dot_hi(l21, l21, NT_DOT))
        i21 = -dot_hi(i22, dot_hi(l21, i11))
        return jnp.concatenate(
            [jnp.concatenate([i11, jnp.zeros((h, h), F32)], axis=1), jnp.concatenate([i21, i22], axis=1)], axis=0
        )
    row = lax.broadcasted_iota(jnp.int32, (n, 2 * n), 0)
    lane = lax.broadcasted_iota(jnp.int32, (n, 2 * n), 1)
    x = jnp.concatenate([a, jnp.where(row == lane, 1.0, 0.0)[:, :n].astype(F32)], axis=1)
    for first in range(0, n, PANEL):
        columns = [jnp.broadcast_to(x[:, j : j + 1], x.shape) for j in range(first, first + PANEL)]
        for i in range(min(PANEL, n - 1 - first)):
            j = first + i
            ratio = jnp.where(row > j, columns[i], 0.0) * (1.0 / columns[i][j : j + 1, :])
            for k in range(i + 1, PANEL):
                columns[k] = columns[k] - ratio * columns[k][j : j + 1, :]
            x = x - ratio * x[j : j + 1, :]
    d = jnp.sum(jnp.where(row == lane, x, 0.0), axis=1, keepdims=True)
    return x[:, n:] * (1.0 / jnp.sqrt(d))


def solve_kernel(g_ref, s_ref, inv_ref, w_ref):
    inv = inverse_factor(g_ref[...])
    inv_ref[...] = inv
    basis = dot_hi(s_ref[...].astype(F32), inv, NT_DOT)
    w_ref[...] = (dot_hi(basis, inv) * 0.125).astype(BF16)


def solve(gram, summed):
    square = pl.BlockSpec((RANK, RANK), lambda j: (0, 0))
    tall = pl.BlockSpec((ROWS, RANK), lambda j: (0, 0))
    return pl.pallas_call(
        solve_kernel,
        grid=(1,),
        in_specs=[VMEM, tall],
        out_specs=[square, tall],
        out_shape=[pltpu.HBM((RANK, RANK), F32), pltpu.HBM((ROWS, RANK), BF16)],
        compiler_params=params(),
        cost_estimate=pl.CostEstimate(flops=2 * 10**10, bytes_accessed=10**6, transcendentals=0),
    )(gram, *in_hbm(summed))


def finish_kernel(held, s_ref, w_ref, inv_ref, t_ref, *refs):
    ins, (err_ref, f_ref, t, a, out, f, w, inv, sem) = refs[:-9], refs[-9:]
    core, m = s_ref[0], s_ref[1]
    if ins[0].shape[1] == HALF:
        parts = [ins[0].at[:, k * CHUNK : (k + 1) * CHUNK] for k in range(CHUNKS)]
    else:
        parts = ins[:CHUNKS]
    small = load([(w_ref, w), (inv_ref, inv)], sem)
    for k in range(CHUNKS):
        if not held:
            load([(t_ref.at[k], t.at[k])], sem, 2 + k)
        load([(parts[k], a.at[k])], sem, 2 + CHUNKS + k)
    t = t_ref if held else t
    at, per = 2 + 2 * CHUNKS, CHUNK // SUB
    for copy in small:
        copy.wait()

    def step(k):
        if not held:
            arrived(t.at[k], sem.at[2 + k])
        arrived(a.at[k], sem.at[2 + CHUNKS + k])
        x = jnp.dot(w[...], t[k].reshape(RANK, CHUNK), preferred_element_type=F32)
        out[k] = (a[k].astype(F32) - x).astype(BF16)
        for s in range(per):
            to = aligned((k * per + s) * BLK + core * SUB, SUB)
            load([(out.at[k, :, s * SUB : (s + 1) * SUB], err_ref.at[:, to])], sem, at + k * per + s)

    rolled(CHUNKS, step)
    x = t[m // per, :, :, aligned(m % per * SUB, SUB)].reshape(RANK, SUB)
    f[...] = dot_hi(inv[...], x.astype(F32)).T * 0.125
    last = load([(f, f_ref.at[aligned(core * SUB, SUB)])], sem, at + CHUNKS * per)

    def sent(k):
        for s in range(per):
            arrived(out.at[k, :, s * SUB : (s + 1) * SUB], sem.at[at + k * per + s])

    rolled(CHUNKS, sent)
    last[0].wait()


def finish(held, where, w, inv, t, parts, before=()):
    n = 4 + len(parts)
    return pl.pallas_call(
        functools.partial(finish_kernel, held),
        in_specs=[SMEM, HBM, HBM, VMEM if held else HBM] + [HBM] * (len(parts) + len(before)),
        out_specs=[HBM, HBM],
        out_shape=[pltpu.HBM((ROWS, COLS), BF16), pltpu.HBM((BLK, RANK), F32)],
        input_output_aliases={n + i: i for i in range(len(before))},
        scratch_shapes=[
            pltpu.VMEM((1 if held else NZ, NM, GROUP, CHUNK), BF16),
            pltpu.VMEM((CHUNKS, ROWS, CHUNK), BF16),
            pltpu.VMEM((CHUNKS, ROWS, CHUNK), BF16),
            pltpu.VMEM((SUB, RANK), F32),
            pltpu.VMEM((ROWS, RANK), BF16),
            pltpu.VMEM((RANK, RANK), F32),
            pltpu.SemaphoreType.DMA((3 + 2 * CHUNKS + NM,)),
        ],
        compiler_params=params(),
        cost_estimate=pl.CostEstimate(flops=2 * ROWS * HALF * RANK, bytes_accessed=4 * ROWS * HALF + 2 * HALF * RANK, transcendentals=0),
    )(where, *in_hbm(w, inv), t if held else in_hbm(t)[0], *in_hbm(*parts, *before))


def swap(x):
    return lax.ppermute(x, "c", [(0, 1), (1, 0)])


def ring_sum(x, axis):
    x1, x3, x2 = (lax.ppermute(x, axis, [(i, (i + k) % 4) for i in range(4)]) for k in (1, 3, 2))
    return (x.astype(F32) + x2.astype(F32)) + (x1.astype(F32) + x3.astype(F32))


def join(c, mine, theirs):
    return jnp.concatenate([pick(c, mine, theirs), pick(c, theirs, mine)], axis=0)


def shards(gradient, error, query):
    gradient, error = gradient[0], error[0]
    c = lax.axis_index("c").astype(jnp.int32)
    m = (lax.axis_index("x") * 4 + lax.axis_index("y")).astype(jnp.int32)
    cv = c.reshape(1)

    with jax.named_scope("query_gather"):
        part = lax.dynamic_slice_in_dim(query, c * SUB, SUB, 0)
        copies = jnp.broadcast_to(part[None], (NM, SUB, RANK))
        half_query = lax.all_to_all(copies, ("x", "y"), 0, 0, tiled=True).reshape(HALF, RANK)

    with jax.named_scope("adjust"):
        own, *others = adjust(cv, gradient, error)
        both = pair(own, [swap(other) for other in others])

    with jax.named_scope("project"):
        keep, give = project(cv, half_query, both)
        chip = (keep + swap(give)).astype(BF16)
        rows = ring_sum(chip, "z").astype(BF16)

    with jax.named_scope("gram"):
        summed, summed_t, gram_x = gram_rows(cv, rows, swap(rows))
        gram_x = ring_sum(gram_x, "x")

    with jax.named_scope("term"):
        pieces = term(summed_t, both).reshape(NZ * NM, RANK // NM, HALF // NZ)
        pieces, gram_x = lax.optimization_barrier((pieces, gram_x))
        pieces = lax.all_to_all(pieces, ("z", "x", "y"), 0, 0, tiled=True)

    with jax.named_scope("gather"):
        gram_y = ring_sum(gram_x.astype(BF16), "y")
        sums, gram_y = lax.optimization_barrier((total(pieces), gram_y))
        mine = lax.all_to_all(sums, ("z", "x", "y"), 0, 0, tiled=True)

    with jax.named_scope("solve"):
        inv, w = solve(join(c, gram_y, swap(gram_y)), summed)
        mine, inv, w = lax.optimization_barrier((mine, inv, w))

    with jax.named_scope("finish"):
        mine = mine.reshape(NZ, NM, GROUP, CHUNK)
        theirs = swap(mine)
        out = finish(True, jnp.stack([c, m]), w, inv, mine, [own])
        new_error, factor = finish(False, jnp.stack([1 - c, m]), w, inv, theirs, others, out)
    return factor, new_error[None]


def solution(mesh):
    grid = Mesh(mesh.devices.reshape(4, 2, 4, 4), ("z", "c", "x", "y"))
    in_specs = (P(("z", "c"), ("x", "y"), None), P(("z", "c"), ("x", "y"), None), P(("x", "y"), None))
    out_specs = (P(("x", "y"), None), P(("z", "c"), ("x", "y"), None))
    return jax.shard_map(shards, mesh=grid, in_specs=in_specs, out_specs=out_specs, check_vma=False)
```

```python
import functools

import jax
import jax.numpy as jnp
from jax import lax
from jax.experimental import pallas as pl
from jax.experimental.pallas import tpu as pltpu
from jax.sharding import Mesh, PartitionSpec as P

BF16 = jnp.bfloat16
F32 = jnp.float32
VMEM_LIMIT = 40 * 1024 * 1024
ROWS, COLS, RANK = 512, 8192, 256
NZ, NM = 4, 16
HALF = COLS // 2
BLK = COLS // NM
SUB = BLK // 2
TN_DOT = (((0,), (0,)), ((), ()))

SMEM = pl.BlockSpec(memory_space=pltpu.SMEM)
VMEM = pl.BlockSpec(memory_space=pltpu.VMEM)
HBM = pl.BlockSpec(memory_space=pltpu.HBM)
CHUNKS = 4
CHUNK = HALF // CHUNKS
STEP = CHUNK // 2
STEPS = HALF // STEP
GROUP = RANK // NM


def params(limit=VMEM_LIMIT):
    return pltpu.CompilerParams(vmem_limit_bytes=limit)


def in_hbm(*arrays):
    return [pltpu.with_memory_space_constraint(x, pltpu.HBM) for x in arrays]


def load(pairs, sem, first=0):
    copies = [pltpu.make_async_copy(src, dst, sem.at[first + i]) for i, (src, dst) in enumerate(pairs)]
    for copy in copies:
        copy.start()
    return copies


def arrived(dst, sem):
    pltpu.make_async_copy(dst, dst, sem).wait()


def rolled(count, step):
    def body(k, carry):
        step(k)
        return carry

    lax.fori_loop(0, count, body, 0)


def aligned(start, size):
    return pl.ds(pl.multiple_of(start, size), size)


def pick(c, first, second):
    return jnp.where(c == 0, first, second)


def adjust_kernel(c_ref, g_ref, d_ref, own_ref, *refs):
    chunks, (g, d, own, other, sem) = refs[:CHUNKS], refs[CHUNKS:]
    for k in range(STEPS):
        cut = slice(2 * k * STEP, 2 * (k + 1) * STEP)
        load([(g_ref.at[:, cut], g.at[k]), (d_ref.at[:, cut], d.at[k])], sem, 2 * k)
    c = c_ref[0]

    def step(k):
        arrived(g.at[k], sem.at[2 * k])
        arrived(d.at[k], sem.at[2 * k + 1])
        for s in range(STEP // SUB):
            part = slice(s * SUB, (s + 1) * SUB)
            for out, core in ((own, c), (other, 1 - c)):
                cut = aligned(s * BLK + core * SUB, SUB)
                out[k, :, part] = (g[k, :, cut].astype(F32) + d[k, :, cut].astype(F32)).astype(BF16)
        load([(own.at[k], own_ref.at[:, aligned(k * STEP, STEP)])], sem, 2 * STEPS + k)
        for i, ref in enumerate(chunks):

            @pl.when(k // 2 == i)
            def _():
                load([(other.at[k], ref.at[:, aligned(k % 2 * STEP, STEP)])], sem, 3 * STEPS + k)

    rolled(STEPS, step)

    def sent(k):
        arrived(own.at[k], sem.at[2 * STEPS + k])
        arrived(other.at[k], sem.at[3 * STEPS + k])

    rolled(STEPS, sent)


def adjust(c, gradient, error):
    return pl.pallas_call(
        adjust_kernel,
        in_specs=[SMEM, HBM, HBM],
        out_specs=[HBM] * (1 + CHUNKS),
        out_shape=[pltpu.HBM((ROWS, HALF), BF16)] + [pltpu.HBM((ROWS, CHUNK), BF16)] * CHUNKS,
        scratch_shapes=[pltpu.VMEM((STEPS, ROWS, 2 * STEP), BF16)] * 2
        + [pltpu.VMEM((STEPS, ROWS, STEP), BF16)] * 2
        + [pltpu.SemaphoreType.DMA((4 * STEPS,))],
        compiler_params=params(),
        cost_estimate=pl.CostEstimate(flops=ROWS * COLS, bytes_accessed=6 * ROWS * COLS, transcendentals=0),
    )(c, *in_hbm(gradient, error))


def pair_kernel(own_ref, *refs):
    chunks, (o_ref, a, b, sem) = refs[:CHUNKS], refs[CHUNKS:]
    for k in range(STEPS):
        part = slice(k % 2 * STEP, (k % 2 + 1) * STEP)
        load([(own_ref.at[:, k * STEP : (k + 1) * STEP], a.at[k]), (chunks[k // 2].at[:, part], b.at[k])], sem, 2 * k)

    def step(k):
        arrived(a.at[k], sem.at[2 * k])
        arrived(b.at[k], sem.at[2 * k + 1])
        a[k] = (a[k].astype(F32) + b[k].astype(F32)).astype(BF16)
        load([(a.at[k], o_ref.at[:, aligned(k * STEP, STEP)])], sem, 2 * STEPS + k)

    rolled(STEPS, step)
    rolled(STEPS, lambda k: arrived(a.at[k], sem.at[2 * STEPS + k]))


def pair(own, chunks):
    return pl.pallas_call(
        pair_kernel,
        in_specs=[HBM] * (1 + CHUNKS),
        out_specs=HBM,
        out_shape=pltpu.HBM((ROWS, HALF), BF16),
        scratch_shapes=[pltpu.VMEM((STEPS, ROWS, STEP), BF16)] * 2 + [pltpu.SemaphoreType.DMA((3 * STEPS,))],
        compiler_params=params(),
        cost_estimate=pl.CostEstimate(flops=ROWS * HALF, bytes_accessed=6 * ROWS * HALF, transcendentals=0),
    )(*in_hbm(own, *chunks))


def project_kernel(c_ref, q_ref, a_ref, keep_ref, give_ref, acc, a, sem):
    for k in range(CHUNKS):
        load([(a_ref.at[:, k * CHUNK : (k + 1) * CHUNK], a.at[k])], sem, k)
    acc[...] = jnp.zeros_like(acc)

    def step(k):
        arrived(a.at[k], sem.at[k])
        acc[...] += jnp.dot(a[k], q_ref[aligned(k * CHUNK, CHUNK), :], preferred_element_type=F32)

    rolled(CHUNKS, step)
    c, h = c_ref[0], ROWS // 2
    keep_ref[...] = acc[aligned(c * h, h), :]
    give_ref[...] = acc[aligned((1 - c) * h, h), :]


def project(c, query, a):
    out = jax.ShapeDtypeStruct((ROWS // 2, RANK), F32)
    return pl.pallas_call(
        project_kernel,
        in_specs=[SMEM, VMEM, HBM],
        out_specs=[VMEM, VMEM],
        out_shape=[out, out],
        scratch_shapes=[
            pltpu.VMEM((ROWS, RANK), F32),
            pltpu.VMEM((CHUNKS, ROWS, CHUNK), BF16),
            pltpu.SemaphoreType.DMA((CHUNKS,)),
        ],
        compiler_params=params(),
        cost_estimate=pl.CostEstimate(flops=2 * ROWS * HALF * RANK, bytes_accessed=2 * ROWS * HALF + 2 * HALF * RANK, transcendentals=0),
    )(c, query, *in_hbm(a))


def gram_kernel(c_ref, mine_ref, theirs_ref, s_ref, st_ref, g_ref):
    c = c_ref[0]
    h = ROWS // 2
    x, y = mine_ref[...], theirs_ref[...]
    s_ref[:h, :] = pick(c, x, y)
    s_ref[h:, :] = pick(c, y, x)
    s = s_ref[...]
    st = s.T
    st_ref[...] = st
    r = RANK // 2
    g_ref[...] = jnp.dot(pick(c, st[:r], st[r:]), s, preferred_element_type=F32).astype(BF16)


def gram_rows(c, mine, theirs):
    return pl.pallas_call(
        gram_kernel,
        grid=(1,),
        in_specs=[SMEM, VMEM, VMEM],
        out_specs=[pl.BlockSpec((ROWS, RANK), lambda j: (0, 0)), VMEM, VMEM],
        out_shape=[
            pltpu.HBM((ROWS, RANK), BF16),
            jax.ShapeDtypeStruct((RANK, ROWS), BF16),
            jax.ShapeDtypeStruct((RANK // 2, RANK), BF16),
        ],
        compiler_params=params(),
        cost_estimate=pl.CostEstimate(flops=2 * ROWS * RANK * RANK, bytes_accessed=4 * ROWS * RANK, transcendentals=0),
    )(c, mine, theirs)


def term_kernel(st_ref, a_ref, t_ref, a, t, sem):
    for k in range(CHUNKS):
        load([(a_ref.at[:, k * CHUNK : (k + 1) * CHUNK], a.at[k])], sem, k)

    def step(k):
        arrived(a.at[k], sem.at[k])
        x = jnp.dot(st_ref[...], a[k], preferred_element_type=F32)
        t[k] = x.astype(BF16).reshape(NM, GROUP, CHUNK)
        load([(t.at[k], t_ref.at[k])], sem, CHUNKS + k)

    rolled(CHUNKS, step)
    rolled(CHUNKS, lambda k: arrived(t.at[k], sem.at[CHUNKS + k]))


def term(st, a):
    return pl.pallas_call(
        term_kernel,
        in_specs=[VMEM, HBM],
        out_specs=HBM,
        out_shape=pltpu.HBM((NZ, NM, GROUP, CHUNK), BF16),
        scratch_shapes=[
            pltpu.VMEM((CHUNKS, ROWS, CHUNK), BF16),
            pltpu.VMEM((NZ, NM, GROUP, CHUNK), BF16),
            pltpu.SemaphoreType.DMA((2 * CHUNKS,)),
        ],
        compiler_params=params(),
        cost_estimate=pl.CostEstimate(flops=2 * ROWS * HALF * RANK, bytes_accessed=2 * ROWS * HALF + 2 * HALF * RANK, transcendentals=0),
    )(st, *in_hbm(a))


def total_kernel(x_ref, o_ref, copy, sem):
    n, k = x_ref.shape[0], copy.shape[0]
    total = jnp.sum(x_ref[...].astype(F32), axis=0).astype(BF16)
    copy[...] = jnp.broadcast_to(total[None], copy.shape)
    for send in load([(copy, o_ref.at[pl.ds(i, k)]) for i in range(0, n, k)], sem):
        send.wait()


def total(pieces):
    k = 16
    return pl.pallas_call(
        total_kernel,
        in_specs=[VMEM],
        out_specs=HBM,
        out_shape=pltpu.HBM(pieces.shape, BF16),
        scratch_shapes=[
            pltpu.VMEM((k,) + pieces.shape[1:], BF16),
            pltpu.SemaphoreType.DMA((pieces.shape[0] // k,)),
        ],
        compiler_params=params(),
        cost_estimate=pl.CostEstimate(flops=pieces.size, bytes_accessed=4 * pieces.size, transcendentals=0),
    )(pieces)


def dot_hi(a, b, dims=(((1,), (0,)), ((), ()))):
    return lax.dot_general(a, b, dims, precision=lax.Precision.HIGHEST, preferred_element_type=F32)


NT_DOT = (((1,), (1,)), ((), ()))
BASE = 64
PANEL = 16
TERMS = 3


def inverse_factor(a):
    n = a.shape[0]
    if n > BASE:
        h = n // 2
        i11 = inverse_factor(a[:h, :h])
        l21 = dot_hi(a[h:, :h], i11, NT_DOT)
        i22 = inverse_factor(a[h:, h:] - dot_hi(l21, l21, NT_DOT))
        i21 = -dot_hi(i22, dot_hi(l21, i11))
        return jnp.concatenate(
            [jnp.concatenate([i11, jnp.zeros((h, h), F32)], axis=1), jnp.concatenate([i21, i22], axis=1)], axis=0
        )
    row = lax.broadcasted_iota(jnp.int32, (n, 2 * n), 0)
    lane = lax.broadcasted_iota(jnp.int32, (n, 2 * n), 1)
    x = jnp.concatenate([a, jnp.where(row == lane, 1.0, 0.0)[:, :n].astype(F32)], axis=1)
    for first in range(0, n, PANEL):
        columns = [jnp.broadcast_to(x[:, j : j + 1], x.shape) for j in range(first, first + PANEL)]
        for i in range(min(PANEL, n - 1 - first)):
            j = first + i
            ratio = jnp.where(row > j, columns[i], 0.0) * (1.0 / columns[i][j : j + 1, :])
            for k in range(i + 1, PANEL):
                columns[k] = columns[k] - ratio * columns[k][j : j + 1, :]
            x = x - ratio * x[j : j + 1, :]
    d = jnp.sum(jnp.where(row == lane, x, 0.0), axis=1, keepdims=True)
    return x[:, n:] * (1.0 / jnp.sqrt(d))


def solve_kernel(g_ref, s_ref, inv_ref, w_ref):
    inv = inverse_factor(g_ref[...])
    rest = inv.T * 0.125
    for i in range(TERMS):
        part = rest.astype(BF16)
        inv_ref[i * RANK : (i + 1) * RANK, :] = part
        rest = rest - part.astype(F32)
    basis = dot_hi(s_ref[...].astype(F32), inv, NT_DOT)
    w_ref[...] = (dot_hi(basis, inv) * 0.125).astype(BF16)


def solve(gram, summed):
    terms = pl.BlockSpec((TERMS * RANK, RANK), lambda j: (0, 0))
    tall = pl.BlockSpec((ROWS, RANK), lambda j: (0, 0))
    return pl.pallas_call(
        solve_kernel,
        grid=(1,),
        in_specs=[VMEM, tall],
        out_specs=[terms, tall],
        out_shape=[pltpu.HBM((TERMS * RANK, RANK), BF16), pltpu.HBM((ROWS, RANK), BF16)],
        compiler_params=params(),
        cost_estimate=pl.CostEstimate(flops=2 * 10**10, bytes_accessed=10**6, transcendentals=0),
    )(gram, *in_hbm(summed))


def finish_kernel(held, s_ref, w_ref, inv_ref, t_ref, *refs):
    ins, (err_ref, f_ref, t, a, out, f, w, inv, sem) = refs[:-9], refs[-9:]
    core, m = s_ref[0], s_ref[1]
    if ins[0].shape[1] == HALF:
        parts = [ins[0].at[:, k * CHUNK : (k + 1) * CHUNK] for k in range(CHUNKS)]
    else:
        parts = ins[:CHUNKS]
    small = load([(w_ref, w), (inv_ref, inv)], sem)
    for k in range(CHUNKS):
        if not held:
            load([(t_ref.at[k], t.at[k])], sem, 2 + k)
        load([(parts[k], a.at[k])], sem, 2 + CHUNKS + k)
    t = t_ref if held else t
    at, per = 2 + 2 * CHUNKS, CHUNK // SUB
    for copy in small:
        copy.wait()

    def step(k):
        if not held:
            arrived(t.at[k], sem.at[2 + k])
        arrived(a.at[k], sem.at[2 + CHUNKS + k])
        x = jnp.dot(w[...], t[k].reshape(RANK, CHUNK), preferred_element_type=F32)
        out[k] = (a[k].astype(F32) - x).astype(BF16)
        for s in range(per):
            to = aligned((k * per + s) * BLK + core * SUB, SUB)
            load([(out.at[k, :, s * SUB : (s + 1) * SUB], err_ref.at[:, to])], sem, at + k * per + s)

    rolled(CHUNKS, step)
    x = t[m // per, :, :, aligned(m % per * SUB, SUB)].reshape(RANK, SUB).T
    f[...] = jnp.dot(x, inv[:RANK, :], preferred_element_type=F32)
    for i in range(1, TERMS):
        f[...] += jnp.dot(x, inv[i * RANK : (i + 1) * RANK, :], preferred_element_type=F32)
    last = load([(f, f_ref.at[aligned(core * SUB, SUB)])], sem, at + CHUNKS * per)

    def sent(k):
        for s in range(per):
            arrived(out.at[k, :, s * SUB : (s + 1) * SUB], sem.at[at + k * per + s])

    rolled(CHUNKS, sent)
    last[0].wait()


def finish(held, where, w, inv, t, parts, before=()):
    n = 4 + len(parts)
    return pl.pallas_call(
        functools.partial(finish_kernel, held),
        in_specs=[SMEM, HBM, HBM, VMEM if held else HBM] + [HBM] * (len(parts) + len(before)),
        out_specs=[HBM, HBM],
        out_shape=[pltpu.HBM((ROWS, COLS), BF16), pltpu.HBM((BLK, RANK), F32)],
        input_output_aliases={n + i: i for i in range(len(before))},
        scratch_shapes=[
            pltpu.VMEM((1 if held else NZ, NM, GROUP, CHUNK), BF16),
            pltpu.VMEM((CHUNKS, ROWS, CHUNK), BF16),
            pltpu.VMEM((CHUNKS, ROWS, CHUNK), BF16),
            pltpu.VMEM((SUB, RANK), F32),
            pltpu.VMEM((ROWS, RANK), BF16),
            pltpu.VMEM((TERMS * RANK, RANK), BF16),
            pltpu.SemaphoreType.DMA((3 + 2 * CHUNKS + NM,)),
        ],
        compiler_params=params(),
        cost_estimate=pl.CostEstimate(flops=2 * ROWS * HALF * RANK, bytes_accessed=4 * ROWS * HALF + 2 * HALF * RANK, transcendentals=0),
    )(where, *in_hbm(w, inv), t if held else in_hbm(t)[0], *in_hbm(*parts, *before))


def swap(x):
    return lax.ppermute(x, "c", [(0, 1), (1, 0)])


def ring_sum(x, axis):
    x1, x3, x2 = (lax.ppermute(x, axis, [(i, (i + k) % 4) for i in range(4)]) for k in (1, 3, 2))
    return (x.astype(F32) + x2.astype(F32)) + (x1.astype(F32) + x3.astype(F32))


def join(c, mine, theirs):
    return jnp.concatenate([pick(c, mine, theirs), pick(c, theirs, mine)], axis=0)


def shards(gradient, error, query):
    gradient, error = gradient[0], error[0]
    c = lax.axis_index("c").astype(jnp.int32)
    m = (lax.axis_index("x") * 4 + lax.axis_index("y")).astype(jnp.int32)
    cv = c.reshape(1)

    with jax.named_scope("query_gather"):
        part = lax.dynamic_slice_in_dim(query, c * SUB, SUB, 0)
        copies = jnp.broadcast_to(part[None], (NM, SUB, RANK))
        half_query = lax.all_to_all(copies, ("x", "y"), 0, 0, tiled=True).reshape(HALF, RANK)

    with jax.named_scope("adjust"):
        own, *others = adjust(cv, gradient, error)
        both = pair(own, [swap(other) for other in others])

    with jax.named_scope("project"):
        keep, give = project(cv, half_query, both)
        chip = (keep + swap(give)).astype(BF16)
        rows = ring_sum(chip, "z").astype(BF16)

    with jax.named_scope("gram"):
        summed, summed_t, gram_x = gram_rows(cv, rows, swap(rows))
        gram_x = ring_sum(gram_x, "x")

    with jax.named_scope("term"):
        pieces = term(summed_t, both).reshape(NZ * NM, RANK // NM, HALF // NZ)
        pieces, gram_x = lax.optimization_barrier((pieces, gram_x))
        pieces = lax.all_to_all(pieces, ("z", "x", "y"), 0, 0, tiled=True)

    with jax.named_scope("gather"):
        gram_y = ring_sum(gram_x.astype(BF16), "y")
        sums, gram_y = lax.optimization_barrier((total(pieces), gram_y))
        mine = lax.all_to_all(sums, ("z", "x", "y"), 0, 0, tiled=True)

    with jax.named_scope("solve"):
        inv, w = solve(join(c, gram_y, swap(gram_y)), summed)
        mine, inv, w = lax.optimization_barrier((mine, inv, w))

    with jax.named_scope("finish"):
        mine = mine.reshape(NZ, NM, GROUP, CHUNK)
        theirs = swap(mine)
        out = finish(True, jnp.stack([c, m]), w, inv, mine, [own])
        new_error, factor = finish(False, jnp.stack([1 - c, m]), w, inv, theirs, others, out)
    return factor, new_error[None]


def solution(mesh):
    grid = Mesh(mesh.devices.reshape(4, 2, 4, 4), ("z", "c", "x", "y"))
    in_specs = (P(("z", "c"), ("x", "y"), None), P(("z", "c"), ("x", "y"), None), P(("x", "y"), None))
    out_specs = (P(("x", "y"), None), P(("z", "c"), ("x", "y"), None))
    return jax.shard_map(shards, mesh=grid, in_specs=in_specs, out_specs=out_specs, check_vma=False)
```

```python
import functools

import jax
import jax.numpy as jnp
from jax import lax
from jax.experimental import pallas as pl
from jax.experimental.pallas import tpu as pltpu
from jax.sharding import Mesh, PartitionSpec as P

BF16 = jnp.bfloat16
F32 = jnp.float32
VMEM_LIMIT = 40 * 1024 * 1024
ROWS, COLS, RANK = 512, 8192, 256
NZ, NM = 4, 16
HALF = COLS // 2
BLK = COLS // NM
SUB = BLK // 2
TN_DOT = (((0,), (0,)), ((), ()))

SMEM = pl.BlockSpec(memory_space=pltpu.SMEM)
VMEM = pl.BlockSpec(memory_space=pltpu.VMEM)
HBM = pl.BlockSpec(memory_space=pltpu.HBM)
CHUNKS = 4
CHUNK = HALF // CHUNKS
STEP = CHUNK // 2
STEPS = HALF // STEP
GROUP = RANK // NM


def params(limit=VMEM_LIMIT):
    return pltpu.CompilerParams(vmem_limit_bytes=limit)


def in_hbm(*arrays):
    return [pltpu.with_memory_space_constraint(x, pltpu.HBM) for x in arrays]


def load(pairs, sem, first=0):
    copies = [pltpu.make_async_copy(src, dst, sem.at[first + i]) for i, (src, dst) in enumerate(pairs)]
    for copy in copies:
        copy.start()
    return copies


def arrived(dst, sem):
    pltpu.make_async_copy(dst, dst, sem).wait()


def rolled(count, step):
    def body(k, carry):
        step(k)
        return carry

    lax.fori_loop(0, count, body, 0)


def aligned(start, size):
    return pl.ds(pl.multiple_of(start, size), size)


def pick(c, first, second):
    return jnp.where(c == 0, first, second)


def adjust_kernel(c_ref, g_ref, d_ref, own_ref, *refs):
    chunks, (g, d, own, other, sem) = refs[:CHUNKS], refs[CHUNKS:]
    for k in range(STEPS):
        cut = slice(2 * k * STEP, 2 * (k + 1) * STEP)
        load([(g_ref.at[:, cut], g.at[k]), (d_ref.at[:, cut], d.at[k])], sem, 2 * k)
    c = c_ref[0]

    def step(k):
        arrived(g.at[k], sem.at[2 * k])
        arrived(d.at[k], sem.at[2 * k + 1])
        for s in range(STEP // SUB):
            part = slice(s * SUB, (s + 1) * SUB)
            for out, core in ((own, c), (other, 1 - c)):
                cut = aligned(s * BLK + core * SUB, SUB)
                out[k, :, part] = (g[k, :, cut].astype(F32) + d[k, :, cut].astype(F32)).astype(BF16)
        load([(own.at[k], own_ref.at[:, aligned(k * STEP, STEP)])], sem, 2 * STEPS + k)
        for i, ref in enumerate(chunks):

            @pl.when(k // 2 == i)
            def _():
                load([(other.at[k], ref.at[:, aligned(k % 2 * STEP, STEP)])], sem, 3 * STEPS + k)

    rolled(STEPS, step)

    def sent(k):
        arrived(own.at[k], sem.at[2 * STEPS + k])
        arrived(other.at[k], sem.at[3 * STEPS + k])

    rolled(STEPS, sent)


def adjust(c, gradient, error):
    return pl.pallas_call(
        adjust_kernel,
        in_specs=[SMEM, HBM, HBM],
        out_specs=[HBM] * (1 + CHUNKS),
        out_shape=[pltpu.HBM((ROWS, HALF), BF16)] + [pltpu.HBM((ROWS, CHUNK), BF16)] * CHUNKS,
        scratch_shapes=[pltpu.VMEM((STEPS, ROWS, 2 * STEP), BF16)] * 2
        + [pltpu.VMEM((STEPS, ROWS, STEP), BF16)] * 2
        + [pltpu.SemaphoreType.DMA((4 * STEPS,))],
        compiler_params=params(),
        cost_estimate=pl.CostEstimate(flops=ROWS * COLS, bytes_accessed=6 * ROWS * COLS, transcendentals=0),
    )(c, *in_hbm(gradient, error))


def pair_kernel(own_ref, *refs):
    chunks, (o_ref, a, b, sem) = refs[:CHUNKS], refs[CHUNKS:]
    for k in range(STEPS):
        part = slice(k % 2 * STEP, (k % 2 + 1) * STEP)
        load([(own_ref.at[:, k * STEP : (k + 1) * STEP], a.at[k]), (chunks[k // 2].at[:, part], b.at[k])], sem, 2 * k)

    def step(k):
        arrived(a.at[k], sem.at[2 * k])
        arrived(b.at[k], sem.at[2 * k + 1])
        a[k] = (a[k].astype(F32) + b[k].astype(F32)).astype(BF16)
        load([(a.at[k], o_ref.at[:, aligned(k * STEP, STEP)])], sem, 2 * STEPS + k)

    rolled(STEPS, step)
    rolled(STEPS, lambda k: arrived(a.at[k], sem.at[2 * STEPS + k]))


def pair(own, chunks):
    return pl.pallas_call(
        pair_kernel,
        in_specs=[HBM] * (1 + CHUNKS),
        out_specs=HBM,
        out_shape=pltpu.HBM((ROWS, HALF), BF16),
        scratch_shapes=[pltpu.VMEM((STEPS, ROWS, STEP), BF16)] * 2 + [pltpu.SemaphoreType.DMA((3 * STEPS,))],
        compiler_params=params(),
        cost_estimate=pl.CostEstimate(flops=ROWS * HALF, bytes_accessed=6 * ROWS * HALF, transcendentals=0),
    )(*in_hbm(own, *chunks))


def project_kernel(c_ref, q_ref, a_ref, keep_ref, give_ref, acc, a, sem):
    for k in range(CHUNKS):
        load([(a_ref.at[:, k * CHUNK : (k + 1) * CHUNK], a.at[k])], sem, k)
    acc[...] = jnp.zeros_like(acc)

    def step(k):
        arrived(a.at[k], sem.at[k])
        acc[...] += jnp.dot(a[k], q_ref[aligned(k * CHUNK, CHUNK), :], preferred_element_type=F32)

    rolled(CHUNKS, step)
    c, h = c_ref[0], ROWS // 2
    keep_ref[...] = acc[aligned(c * h, h), :]
    give_ref[...] = acc[aligned((1 - c) * h, h), :].astype(BF16)


def project(c, query, a):
    out = jax.ShapeDtypeStruct((ROWS // 2, RANK), F32)
    return pl.pallas_call(
        project_kernel,
        in_specs=[SMEM, VMEM, HBM],
        out_specs=[VMEM, VMEM],
        out_shape=[out, jax.ShapeDtypeStruct(out.shape, BF16)],
        scratch_shapes=[
            pltpu.VMEM((ROWS, RANK), F32),
            pltpu.VMEM((CHUNKS, ROWS, CHUNK), BF16),
            pltpu.SemaphoreType.DMA((CHUNKS,)),
        ],
        compiler_params=params(),
        cost_estimate=pl.CostEstimate(flops=2 * ROWS * HALF * RANK, bytes_accessed=2 * ROWS * HALF + 2 * HALF * RANK, transcendentals=0),
    )(c, query, *in_hbm(a))


def gram_kernel(c_ref, mine_ref, theirs_ref, s_ref, st_ref, g_ref):
    c = c_ref[0]
    h = ROWS // 2
    x, y = mine_ref[...], theirs_ref[...]
    s_ref[:h, :] = pick(c, x, y)
    s_ref[h:, :] = pick(c, y, x)
    s = s_ref[...]
    st = s.T
    st_ref[...] = st
    r = RANK // 2
    g_ref[...] = jnp.dot(pick(c, st[:r], st[r:]), s, preferred_element_type=F32).astype(BF16)


def gram_rows(c, mine, theirs):
    return pl.pallas_call(
        gram_kernel,
        grid=(1,),
        in_specs=[SMEM, VMEM, VMEM],
        out_specs=[pl.BlockSpec((ROWS, RANK), lambda j: (0, 0)), VMEM, VMEM],
        out_shape=[
            pltpu.HBM((ROWS, RANK), BF16),
            jax.ShapeDtypeStruct((RANK, ROWS), BF16),
            jax.ShapeDtypeStruct((RANK // 2, RANK), BF16),
        ],
        compiler_params=params(),
        cost_estimate=pl.CostEstimate(flops=2 * ROWS * RANK * RANK, bytes_accessed=4 * ROWS * RANK, transcendentals=0),
    )(c, mine, theirs)


def term_kernel(st_ref, a_ref, t_ref, a, t, sem):
    for k in range(CHUNKS):
        load([(a_ref.at[:, k * CHUNK : (k + 1) * CHUNK], a.at[k])], sem, k)

    def step(k):
        arrived(a.at[k], sem.at[k])
        x = jnp.dot(st_ref[...], a[k], preferred_element_type=F32)
        t[k] = x.astype(BF16).reshape(NM, GROUP, CHUNK)
        load([(t.at[k], t_ref.at[k])], sem, CHUNKS + k)

    rolled(CHUNKS, step)
    rolled(CHUNKS, lambda k: arrived(t.at[k], sem.at[CHUNKS + k]))


def term(st, a):
    return pl.pallas_call(
        term_kernel,
        in_specs=[VMEM, HBM],
        out_specs=HBM,
        out_shape=pltpu.HBM((NZ, NM, GROUP, CHUNK), BF16),
        scratch_shapes=[
            pltpu.VMEM((CHUNKS, ROWS, CHUNK), BF16),
            pltpu.VMEM((NZ, NM, GROUP, CHUNK), BF16),
            pltpu.SemaphoreType.DMA((2 * CHUNKS,)),
        ],
        compiler_params=params(),
        cost_estimate=pl.CostEstimate(flops=2 * ROWS * HALF * RANK, bytes_accessed=2 * ROWS * HALF + 2 * HALF * RANK, transcendentals=0),
    )(st, *in_hbm(a))


def total_kernel(x_ref, o_ref, copy, sem):
    n, k = x_ref.shape[0], copy.shape[0]
    total = jnp.sum(x_ref[...].astype(F32), axis=0).astype(BF16)
    copy[...] = jnp.broadcast_to(total[None], copy.shape)
    for send in load([(copy, o_ref.at[pl.ds(i, k)]) for i in range(0, n, k)], sem):
        send.wait()


def total(pieces):
    k = 16
    return pl.pallas_call(
        total_kernel,
        in_specs=[VMEM],
        out_specs=HBM,
        out_shape=pltpu.HBM(pieces.shape, BF16),
        scratch_shapes=[
            pltpu.VMEM((k,) + pieces.shape[1:], BF16),
            pltpu.SemaphoreType.DMA((pieces.shape[0] // k,)),
        ],
        compiler_params=params(),
        cost_estimate=pl.CostEstimate(flops=pieces.size, bytes_accessed=4 * pieces.size, transcendentals=0),
    )(pieces)


def dot_hi(a, b, dims=(((1,), (0,)), ((), ()))):
    return lax.dot_general(a, b, dims, precision=lax.Precision.HIGHEST, preferred_element_type=F32)


NT_DOT = (((1,), (1,)), ((), ()))
BASE = 64
PANEL = 16
TERMS = 3


def inverse_factor(a):
    n = a.shape[0]
    if n > BASE:
        h = n // 2
        i11 = inverse_factor(a[:h, :h])
        l21 = dot_hi(a[h:, :h], i11, NT_DOT)
        i22 = inverse_factor(a[h:, h:] - dot_hi(l21, l21, NT_DOT))
        i21 = -dot_hi(i22, dot_hi(l21, i11))
        return jnp.concatenate(
            [jnp.concatenate([i11, jnp.zeros((h, h), F32)], axis=1), jnp.concatenate([i21, i22], axis=1)], axis=0
        )
    row = lax.broadcasted_iota(jnp.int32, (n, 2 * n), 0)
    lane = lax.broadcasted_iota(jnp.int32, (n, 2 * n), 1)
    x = jnp.concatenate([a, jnp.where(row == lane, 1.0, 0.0)[:, :n].astype(F32)], axis=1)
    for first in range(0, n, PANEL):
        columns = [jnp.broadcast_to(x[:, j : j + 1], x.shape) for j in range(first, first + PANEL)]
        for i in range(min(PANEL, n - 1 - first)):
            j = first + i
            ratio = jnp.where(row > j, columns[i], 0.0) * (1.0 / columns[i][j : j + 1, :])
            for k in range(i + 1, PANEL):
                columns[k] = columns[k] - ratio * columns[k][j : j + 1, :]
            x = x - ratio * x[j : j + 1, :]
    d = jnp.sum(jnp.where(row == lane, x, 0.0), axis=1, keepdims=True)
    return x[:, n:] * (1.0 / jnp.sqrt(d))


def solve_kernel(g_ref, s_ref, inv_ref, w_ref):
    inv = inverse_factor(g_ref[...])
    rest = inv.T * 0.125
    for i in range(TERMS):
        part = rest.astype(BF16)
        inv_ref[i * RANK : (i + 1) * RANK, :] = part
        rest = rest - part.astype(F32)
    basis = dot_hi(s_ref[...].astype(F32), inv, NT_DOT)
    w_ref[...] = (dot_hi(basis, inv) * 0.125).astype(BF16)


def solve(gram, summed):
    terms = pl.BlockSpec((TERMS * RANK, RANK), lambda j: (0, 0))
    tall = pl.BlockSpec((ROWS, RANK), lambda j: (0, 0))
    return pl.pallas_call(
        solve_kernel,
        grid=(1,),
        in_specs=[VMEM, tall],
        out_specs=[terms, tall],
        out_shape=[pltpu.HBM((TERMS * RANK, RANK), BF16), pltpu.HBM((ROWS, RANK), BF16)],
        compiler_params=params(),
        cost_estimate=pl.CostEstimate(flops=2 * 10**10, bytes_accessed=10**6, transcendentals=0),
    )(gram, *in_hbm(summed))


def finish_kernel(held, s_ref, w_ref, inv_ref, t_ref, *refs):
    ins, (err_ref, f_ref, t, a, out, f, w, inv, sem) = refs[:-9], refs[-9:]
    core, m = s_ref[0], s_ref[1]
    if ins[0].shape[1] == HALF:
        parts = [ins[0].at[:, k * CHUNK : (k + 1) * CHUNK] for k in range(CHUNKS)]
    else:
        parts = ins[:CHUNKS]
    small = load([(w_ref, w), (inv_ref, inv)], sem)
    for k in range(CHUNKS):
        if not held:
            load([(t_ref.at[k], t.at[k])], sem, 2 + k)
        load([(parts[k], a.at[k])], sem, 2 + CHUNKS + k)
    t = t_ref if held else t
    at, per = 2 + 2 * CHUNKS, CHUNK // SUB
    for copy in small:
        copy.wait()

    def step(k):
        if not held:
            arrived(t.at[k], sem.at[2 + k])
        arrived(a.at[k], sem.at[2 + CHUNKS + k])
        x = jnp.dot(w[...], t[k].reshape(RANK, CHUNK), preferred_element_type=F32)
        out[k] = (a[k].astype(F32) - x).astype(BF16)
        for s in range(per):
            to = aligned((k * per + s) * BLK + core * SUB, SUB)
            load([(out.at[k, :, s * SUB : (s + 1) * SUB], err_ref.at[:, to])], sem, at + k * per + s)

    rolled(CHUNKS, step)
    x = t[m // per, :, :, aligned(m % per * SUB, SUB)].reshape(RANK, SUB).T
    f[...] = jnp.dot(x, inv[:RANK, :], preferred_element_type=F32)
    for i in range(1, TERMS):
        f[...] += jnp.dot(x, inv[i * RANK : (i + 1) * RANK, :], preferred_element_type=F32)
    last = load([(f, f_ref.at[aligned(core * SUB, SUB)])], sem, at + CHUNKS * per)

    def sent(k):
        for s in range(per):
            arrived(out.at[k, :, s * SUB : (s + 1) * SUB], sem.at[at + k * per + s])

    rolled(CHUNKS, sent)
    last[0].wait()


def finish(held, where, w, inv, t, parts, before=()):
    n = 4 + len(parts)
    return pl.pallas_call(
        functools.partial(finish_kernel, held),
        in_specs=[SMEM, HBM, HBM, VMEM if held else HBM] + [HBM] * (len(parts) + len(before)),
        out_specs=[HBM, HBM],
        out_shape=[pltpu.HBM((ROWS, COLS), BF16), pltpu.HBM((BLK, RANK), F32)],
        input_output_aliases={n + i: i for i in range(len(before))},
        scratch_shapes=[
            pltpu.VMEM((1 if held else NZ, NM, GROUP, CHUNK), BF16),
            pltpu.VMEM((CHUNKS, ROWS, CHUNK), BF16),
            pltpu.VMEM((CHUNKS, ROWS, CHUNK), BF16),
            pltpu.VMEM((SUB, RANK), F32),
            pltpu.VMEM((ROWS, RANK), BF16),
            pltpu.VMEM((TERMS * RANK, RANK), BF16),
            pltpu.SemaphoreType.DMA((3 + 2 * CHUNKS + NM,)),
        ],
        compiler_params=params(),
        cost_estimate=pl.CostEstimate(flops=2 * ROWS * HALF * RANK, bytes_accessed=4 * ROWS * HALF + 2 * HALF * RANK, transcendentals=0),
    )(where, *in_hbm(w, inv), t if held else in_hbm(t)[0], *in_hbm(*parts, *before))


def swap(x):
    return lax.ppermute(x, "c", [(0, 1), (1, 0)])


def ring_sum(x, axis):
    x1, x3, x2 = (lax.ppermute(x, axis, [(i, (i + k) % 4) for i in range(4)]) for k in (1, 3, 2))
    return (x.astype(F32) + x2.astype(F32)) + (x1.astype(F32) + x3.astype(F32))


def join(c, mine, theirs):
    return jnp.concatenate([pick(c, mine, theirs), pick(c, theirs, mine)], axis=0)


def shards(gradient, error, query):
    gradient, error = gradient[0], error[0]
    c = lax.axis_index("c").astype(jnp.int32)
    m = (lax.axis_index("x") * 4 + lax.axis_index("y")).astype(jnp.int32)
    cv = c.reshape(1)

    with jax.named_scope("query_gather"):
        part = lax.dynamic_slice_in_dim(query, c * SUB, SUB, 0)
        copies = jnp.broadcast_to(part[None], (NM, SUB, RANK))
        half_query = lax.all_to_all(copies, ("x", "y"), 0, 0, tiled=True).reshape(HALF, RANK)

    with jax.named_scope("adjust"):
        own, *others = adjust(cv, gradient, error)
        both = pair(own, [swap(other) for other in others])

    with jax.named_scope("project"):
        keep, give = project(cv, half_query, both)
        chip = (keep + swap(give)).astype(BF16)
        rows = ring_sum(chip, "z").astype(BF16)

    with jax.named_scope("gram"):
        summed, summed_t, gram_x = gram_rows(cv, rows, swap(rows))
        gram_x = ring_sum(gram_x, "x")

    with jax.named_scope("term"):
        pieces = term(summed_t, both).reshape(NZ * NM, RANK // NM, HALF // NZ)
        pieces, gram_x = lax.optimization_barrier((pieces, gram_x))
        pieces = lax.all_to_all(pieces, ("z", "x", "y"), 0, 0, tiled=True)

    with jax.named_scope("gather"):
        gram_y = ring_sum(gram_x.astype(BF16), "y")
        sums, gram_y = lax.optimization_barrier((total(pieces), gram_y))
        mine = lax.all_to_all(sums, ("z", "x", "y"), 0, 0, tiled=True)

    with jax.named_scope("solve"):
        inv, w = solve(join(c, gram_y, swap(gram_y)), summed)
        mine, inv, w = lax.optimization_barrier((mine, inv, w))

    with jax.named_scope("finish"):
        mine = mine.reshape(NZ, NM, GROUP, CHUNK)
        theirs = swap(mine)
        out = finish(True, jnp.stack([c, m]), w, inv, mine, [own])
        new_error, factor = finish(False, jnp.stack([1 - c, m]), w, inv, theirs, others, out)
    return factor, new_error[None]


def solution(mesh):
    grid = Mesh(mesh.devices.reshape(4, 2, 4, 4), ("z", "c", "x", "y"))
    in_specs = (P(("z", "c"), ("x", "y"), None), P(("z", "c"), ("x", "y"), None), P(("x", "y"), None))
    out_specs = (P(("x", "y"), None), P(("z", "c"), ("x", "y"), None))
    return jax.shard_map(shards, mesh=grid, in_specs=in_specs, out_specs=out_specs, check_vma=False)
```
